256 devices in a mesh: row: 8 (over x_hi, y), col: 8 (over z), scene: 4 (over x_lo, core).
Axes of the slice: x: 4 (x_hi: 2, x_lo: 2; x = x_hi * 2 + x_lo), y: 4, z: 8, core: 2. Of those that a mesh axis runs over, the one named last changes fastest.
Arguments:
- features: bfloat16 [8, 112, 112, 384], P('scene', 'row', 'col'), may hold values from -6 to 6
- grad_out: bfloat16 [8, 112, 112, 384], P('scene', 'row', 'col'), may hold values from -6 to 6
- norm_gain: float32 [384], replicated, may hold values from 0.1 to 1.9
- norm_shift: float32 [384], replicated, may hold values from -3 to 3
- qkv_weight: bfloat16 [384, 1152], replicated, may hold values from -0.3125 to 0.3125
- qkv_bias: float32 [1152], replicated, may hold values from -3 to 3
- proj_weight: bfloat16 [384, 384], replicated, may hold values from -0.3125 to 0.3125
- bias_table: float32 [169, 12], replicated, may hold values from -8 to 320
Outputs:
- grad_x: bfloat16 [8, 112, 112, 384], P('scene', 'row', 'col')
- grad_gain: float32 [384], replicated
- grad_shift: float32 [384], replicated
- grad_wqkv: float32 [384, 1152], replicated
- grad_bqkv: float32 [1152], replicated
- grad_wproj: float32 [384, 384], replicated
- grad_bproj: float32 [384], replicated
- grad_table: float32 [169, 12], replicated
The draws below stay inside these ranges and needn't reach their ends.
All inputs are finite; a program needn't handle non-finite values.
Results may differ from the reference program's by a relative error of at most 0.025.
Values may be sent and summed in bfloat16 or wider, within the bound.
A program may use at most 64 MiB of HBM per device.

```python
import math
import jax
import jax.numpy as jnp
from jax import lax

C = 384
HEADS = 12
WIN = 7
SHIFT = 3
H = 112
W = 112
SCENES = 8
TABLE = 169


def draw_bias_table(key, part):
    key = jax.random.fold_in(key, 17)
    keys_list = jax.random.split(key, 1)
    table_values = jnp.clip(jax.random.normal(keys_list[0], (TABLE, HEADS), jnp.float32), -6.0, 6.0)
    return table_values.astype(jnp.float32)


def steps_of(own_key, extent, cuts, low, largest):
    def one(dim, parts):
        draws = jax.random.uniform(jax.random.fold_in(jax.random.fold_in(own_key, 6), dim), (parts,), jnp.float32, low / len(cuts), largest / len(cuts))
        return jnp.repeat(jnp.exp(draws), extent[dim] // parts).reshape((-1,) + (1,) * (len(extent) - dim - 1))

    gain = one(*cuts[0])
    for cut in cuts[1:]:
        gain = gain * one(*cut)
    return gain


def normal_values(rng, extent, width, reach, cuts=(), kind=jnp.bfloat16):
    level = steps_of(rng, extent, cuts, -0.22, 0.18) if cuts else 1.0
    array = jax.random.normal(rng, extent, jnp.float32) * width * level
    return jnp.minimum(jnp.maximum(array, -reach), reach).astype(kind)


def setup_inputs(seed: int = 0) -> dict:
    key_of = jax.random.split(jax.random.key(seed), 9)
    features = normal_values(key_of[0], (SCENES, H, W, C), 1.0, 6.0, ((0, 4), (1, 8), (2, 8)))
    grad_out = normal_values(key_of[1], (SCENES, H, W, C), 1.0, 6.0, ((0, 4), (1, 8), (2, 8)))
    norm_gain = jnp.clip(1.0 + 0.18 * jax.random.normal(key_of[2], (C,), jnp.float32), 0.1, 1.9)
    norm_shift = normal_values(key_of[3], (C,), 0.5, 3.0, (), jnp.float32)
    qkv_weight = normal_values(key_of[4], (C, 3 * C), C ** -0.5, 0.3125)
    qkv_bias = normal_values(key_of[5], (3 * C,), 0.5, 3.0, (), jnp.float32)
    proj_weight = normal_values(key_of[6], (C, C), C ** -0.5, 0.3125)
    bias_table = draw_bias_table(jax.random.fold_in(key_of[8], 71), 0)
    return dict(features=features, grad_out=grad_out, norm_gain=norm_gain, norm_shift=norm_shift, qkv_weight=qkv_weight, qkv_bias=qkv_bias, proj_weight=proj_weight, bias_table=bias_table)


NORM_EPS = 1e-05
MASKED_SCORE = -1e+30

def layer_norm(tokens, norm_gain, norm_shift):
    values = tokens.astype(jnp.float32)
    average = lax.optimization_barrier(jnp.mean(values, axis=-1, keepdims=True))
    centered = values - average
    variance = lax.optimization_barrier(jnp.mean(centered * centered, axis=-1, keepdims=True))
    return (centered * lax.rsqrt(variance + NORM_EPS) * norm_gain + norm_shift).astype(jnp.bfloat16)

def to_windows(grid, side):
    scene_count, row_count, col_count, chan_count = grid.shape
    grid = grid.reshape(scene_count, row_count // side, side, col_count // side, side, chan_count)
    grid = grid.transpose(0, 1, 3, 2, 4, 5)
    return grid.reshape(-1, side * side, chan_count)

def from_windows(windows, side, scene_count, row_count, col_count):
    chan_count = windows.shape[-1]
    grid = windows.reshape(scene_count, row_count // side, col_count // side, side, side, chan_count)
    grid = grid.transpose(0, 1, 3, 2, 4, 5)
    return grid.reshape(scene_count, row_count, col_count, chan_count)

def band_of(places, total):
    return (places >= total - WIN).astype(jnp.int32) + (places >= total - SHIFT).astype(jnp.int32)

def relative_bias(bias_table, side):
    cell_count = side * side
    places = jnp.arange(cell_count, dtype=jnp.int32)
    row_of = places // side
    col_of = places % side
    index_grid = (row_of[:, None] - row_of[None, :] + side - 1) * (2 * side - 1) + (col_of[:, None] - col_of[None, :] + side - 1)
    offsets = jnp.arange(bias_table.shape[0], dtype=jnp.int32)
    one_hot = (index_grid[:, :, None] == offsets[None, None, :]).astype(jnp.float32)
    return jnp.einsum('qkt,th->hqk', one_hot, bias_table, precision=lax.Precision.HIGHEST)

def window_attention(qkv_win, bias_table, region_win, side):
    win_count, cell_count, triple = qkv_win.shape
    heads_count = bias_table.shape[1]
    chan_count = triple // 3
    head_size = chan_count // heads_count
    split_parts = qkv_win.astype(jnp.float32).reshape(win_count, cell_count, 3, heads_count, head_size)
    queries = split_parts[:, :, 0]
    keys_all = split_parts[:, :, 1]
    values = split_parts[:, :, 2]
    scores = jnp.einsum('bqhd,bkhd->bhqk', queries, keys_all, precision=lax.Precision.HIGHEST) * head_size ** (-0.5)
    scores = scores + relative_bias(bias_table, side)[None]
    same_region = region_win[:, None, :, None] == region_win[:, None, None, :]
    scores = jnp.where(same_region, scores, MASKED_SCORE)
    weights = jax.nn.softmax(scores, axis=-1).astype(jnp.bfloat16)
    mixed_heads = jnp.einsum('bhqk,bkhd->bqhd', weights.astype(jnp.float32), values, precision=lax.Precision.HIGHEST)
    return mixed_heads.reshape(win_count, cell_count, chan_count).astype(jnp.bfloat16)

def local_backward(shifted, upstream, region, norm_gain, norm_shift, qkv_weight, qkv_bias, proj_weight, bias_table):
    scene_count, row_count, col_count, chan_count = shifted.shape
    flat = shifted.reshape(-1, chan_count)
    normed, norm_back = jax.vjp(layer_norm, flat, norm_gain, norm_shift)
    qkv = (jnp.dot(normed, qkv_weight, preferred_element_type=jnp.float32) + qkv_bias).astype(jnp.bfloat16)
    qkv_win = to_windows(qkv.reshape(scene_count, row_count, col_count, 3 * chan_count), WIN)
    region_win = to_windows(region[..., None], WIN)[..., 0]

    def attend(qkv_in, table_in):
        return window_attention(qkv_in, table_in, region_win, WIN)
    attn_win, attn_back = jax.vjp(attend, qkv_win, bias_table)
    attended = from_windows(attn_win, WIN, scene_count, row_count, col_count).reshape(-1, chan_count)
    incoming = upstream.reshape(-1, chan_count)
    grad_wproj = jnp.dot(attended.T, incoming, preferred_element_type=jnp.float32)
    grad_bproj = lax.optimization_barrier(jnp.sum(incoming.astype(jnp.float32), axis=0))
    grad_attn = jnp.dot(incoming, proj_weight.T, preferred_element_type=jnp.float32).astype(jnp.bfloat16)
    grad_attn_win = to_windows(grad_attn.reshape(scene_count, row_count, col_count, chan_count), WIN)
    grad_qkv_win, grad_table = attn_back(grad_attn_win)
    grad_qkv = from_windows(grad_qkv_win, WIN, scene_count, row_count, col_count).reshape(-1, 3 * chan_count)
    grad_wqkv = jnp.dot(normed.T, grad_qkv, preferred_element_type=jnp.float32)
    grad_bqkv = lax.optimization_barrier(jnp.sum(grad_qkv.astype(jnp.float32), axis=0))
    grad_normed = jnp.dot(grad_qkv, qkv_weight.T, preferred_element_type=jnp.float32).astype(jnp.bfloat16)
    grad_flat, grad_gain, grad_shift = norm_back(grad_normed)
    grad_shifted = grad_flat.reshape(scene_count, row_count, col_count, chan_count)
    return (grad_shifted, (grad_gain, grad_shift, grad_wqkv, grad_bqkv, grad_wproj, grad_bproj, grad_table))

def reference(features, grad_out, norm_gain, norm_shift, qkv_weight, qkv_bias, proj_weight, bias_table):
    row_band = band_of(jnp.arange(H, dtype=jnp.int32), H)
    col_band = band_of(jnp.arange(W, dtype=jnp.int32), W)
    region = (3 * row_band[:, None] + col_band[None, :]).astype(jnp.int32)

    def one_scene(scene_items):
        scene_feat, scene_grad = scene_items
        shifted = jnp.roll(scene_feat, (-SHIFT, -SHIFT), (0, 1))[None]
        upstream = jnp.roll(scene_grad, (-SHIFT, -SHIFT), (0, 1))[None]
        grad_shifted, partial_sums = local_backward(shifted, upstream, region[None], norm_gain, norm_shift, qkv_weight, qkv_bias, proj_weight, bias_table)
        restored = jnp.roll(grad_shifted[0], (SHIFT, SHIFT), (0, 1))
        grad_scene = (scene_grad.astype(jnp.float32) + restored.astype(jnp.float32)).astype(jnp.bfloat16)
        return (grad_scene, partial_sums)
    grad_x, partial_sums = lax.map(one_scene, (features, grad_out))
    scale = 1.0 / math.sqrt(SCENES * H * W)
    totals = [lax.optimization_barrier(jnp.sum(member, axis=0)) * scale for member in partial_sums]
    return (grad_x, totals[0], totals[1], totals[2], totals[3], totals[4], totals[5], totals[6])
```

```python
import functools
import math

import jax
import jax.numpy as jnp
import numpy as np
from jax import lax
from jax.experimental import pallas as pl
from jax.experimental.pallas import tpu as pltpu
from jax.sharding import PartitionSpec as P
MESH = pl.DeviceIdType.MESH
f32, bf16 = jnp.float32, jnp.bfloat16
CH = 10

def place():
    row, z, scene = lax.axis_index("row"), lax.axis_index("col"), lax.axis_index("scene")
    x = (row // 4) * 2 + scene // 2
    return x, row % 4, z, scene % 2

def at(x, y, z, core):
    return ((x // 2) * 4 + y, z, (x % 2) * 2 + core)

def pack(total):
    big = total[:9].astype(bf16)
    t = total[9, :8] + total[9, 8:]
    hi = t.astype(bf16).astype(f32)
    small = jnp.concatenate([hi, t - hi], axis=0).astype(bf16)
    return big, small

def reduce_kernel(stop, g, h, out, hout, r0, s1, r1, s2, r2, acc,
                  h_s, h_r, p0s, p0r, p1s, p1r, p2s, p2r, p3s, p3r, p4s, p4r, p5s, p5r):
    x, y, z, core = place()
    me = x * 4 + y
    row, scene = lax.axis_index("row"), lax.axis_index("scene")
    def plane(k):
        return lax.rem(x + k // 4, 4), lax.rem(y + k % 4, 4)
    bar = pltpu.get_barrier_semaphore()
    def greet(dev):
        pl.semaphore_signal(bar, inc=1, device_id=dev, device_id_type=MESH)
    greet(at(x, y, z, 1 - core))
    for k in range(1, 16):
        px, py = plane(k)
        greet(at(px, py, z, core))
    for k in range(1, 8):
        greet(at(x, y, lax.rem(z + k, 8), core))
    rm, zm = lax.rem(row + 7, 8), lax.rem(z + 7, 8)
    rp, zp = lax.rem(row + 1, 8), lax.rem(z + 1, 8)
    for d in ((rm, z, scene), (row, zm, scene), (rm, zm, scene)):
        greet(d)
    pl.semaphore_wait(bar, 1 + 15 + 7 + 3)

    def rc(src, dst, ss, rs, dev):
        return pltpu.make_async_remote_copy(src_ref=src, dst_ref=dst, send_sem=ss, recv_sem=rs, device_id=dev, device_id_type=MESH)
    sib = at(x, y, z, 1 - core)
    pend = []
    def chunk(k):
        return lax.rem(me // 4 + k // 4, 4) * 4 + lax.rem(me % 4 + k % 4, 4)
    order = list(range(1, 16)) + [0]
    c0 = [None] * 16
    for k in order:
        c = chunk(k)
        c0[k] = rc(g.at[(1 - core) * 16 + c], r0.at[c], p0s.at[k], p0r.at[k], sib)
        c0[k].start()
    hc = []
    for i, (d, lo, n) in enumerate((((rp, z, scene), 0, 80), ((row, zp, scene), 80, 80), ((rp, zp, scene), 160, 32))):
        cp = rc(h.at[pl.ds(lo, n)], hout.at[pl.ds(lo, n)], h_s.at[i], h_r.at[i], d)
        cp.start()
        hc.append(cp)
    c1 = [None] * 16
    for k in order:
        c = chunk(k)
        c0[k].wait_recv()
        total = g[core * 16 + c].astype(f32) + r0[c].astype(f32)
        if k:
            big, small = pack(total)
            s1[c, :9] = big
            s1[c, 9] = small
            if stop >= 1:
                px, py = plane(k)
                c1[k] = rc(s1.at[c], r1.at[k], p1s.at[k], p1r.at[k], at(px, py, z, core))
                c1[k].start()
        else:
            acc[...] = total
    if stop >= 1:
        for k in range(1, 16):
            c1[k].wait_recv()
            acc[...] += r1[k].astype(f32)
    big, small = pack(acc[...])
    for t in range(8):
        s2[t, 0] = big[t]
        s2[t, 1] = big[8]
        s2[t, 2] = small
    c2, c3 = [None] * 8, [None] * 8
    if stop >= 2:
        for k in range(1, 8):
            d = lax.rem(z + k, 8)
            c2[k] = rc(s2.at[d], r2.at[z], p2s.at[k], p2r.at[k], at(x, y, d, core))
            c2[k].start()
        r2[z] = s2[z]
        for k in range(1, 8):
            fr = lax.rem(z + 8 - k, 8)
            rc(s2.at[fr], r2.at[fr], p2s.at[k], p2r.at[k], at(x, y, fr, core)).wait_recv()
        t3 = r2[0].astype(f32)
        for t in range(1, 8):
            t3 += r2[t].astype(f32)
        tt = t3[2, :8] + t3[2, 8:]
        hi = tt.astype(bf16).astype(f32)
        mine = core * 16 + me
        out[mine, z] = t3[0].astype(bf16)
        out[mine, 8] = t3[1].astype(bf16)
        out[mine, 9] = jnp.concatenate([hi, tt - hi], axis=0).astype(bf16)
        for k in range(1, 8):
            d = lax.rem(z + k, 8)
            c3[k] = rc(out.at[mine, z], out.at[mine, z], p3s.at[k], p3r.at[k], at(x, y, d, core))
            c3[k].start()
        for k in range(1, 8):
            fr = lax.rem(z + 8 - k, 8)
            rc(out.at[mine, fr], out.at[mine, fr], p3s.at[k], p3r.at[k], at(x, y, fr, core)).wait_recv()
    c4, c5 = [None] * 16, [None] * 16
    if stop >= 3:
        mine = core * 16 + me
        for k in range(1, 16):
            px, py = plane(k)
            c4[k] = rc(out.at[mine], out.at[mine], p4s.at[k], p4r.at[k], at(px, py, z, core))
            c4[k].start()
        if stop >= 4:
            c5[0] = rc(out.at[mine], out.at[mine], p5s.at[0], p5r.at[0], sib)
            c5[0].start()
        for k in range(1, 16):
            fx, fy = lax.rem(x + 4 - k // 4, 4), lax.rem(y + 4 - k % 4, 4)
            f = core * 16 + fx * 4 + fy
            rc(out.at[f], out.at[f], p4s.at[k], p4r.at[k], at(fx, fy, z, core)).wait_recv()
            if stop >= 4:
                c5[k] = rc(out.at[f], out.at[f], p5s.at[k], p5r.at[k], sib)
                c5[k].start()
        if stop >= 4:
            for k in range(16):
                fx, fy = lax.rem(x + 4 - k // 4, 4), lax.rem(y + 4 - k % 4, 4)
                f = (1 - core) * 16 + fx * 4 + fy
                rc(out.at[f], out.at[f], p5s.at[k], p5r.at[k], sib).wait_recv()
    for cp in hc:
        cp.wait_recv()
    for cp in hc + c0 + c1 + c2 + c3 + c4 + c5:
        if cp is not None:
            cp.wait_send()

def reduce_all(g, h, stop=4):
    V = pl.BlockSpec(memory_space=pltpu.VMEM)
    D = pltpu.SemaphoreType.DMA
    return pl.pallas_call(
        functools.partial(reduce_kernel, stop),
        out_shape=(jax.ShapeDtypeStruct((32, CH, 16, 128), bf16), jax.ShapeDtypeStruct((192, 384), bf16)),
        in_specs=[V, V], out_specs=(V, V),
        scratch_shapes=[
            pltpu.VMEM((16, CH, 16, 128), bf16), pltpu.VMEM((16, CH, 16, 128), bf16), pltpu.VMEM((16, CH, 16, 128), bf16),
            pltpu.VMEM((8, 3, 16, 128), bf16), pltpu.VMEM((8, 3, 16, 128), bf16), pltpu.VMEM((CH, 16, 128), f32),
            D((3,)), D((3,)), D((16,)), D((16,)), D((16,)), D((16,)), D((8,)), D((8,)), D((8,)), D((8,)), D((16,)), D((16,)), D((16,)), D((16,)),
        ],
        compiler_params=pltpu.CompilerParams(collective_id=1, has_side_effects=True, vmem_limit_bytes=48 << 20),
    )(g, h)


WIN, SHIFT, NORM_EPS, MASKED = 7, 3, 1e-05, -1e30
LOG2E = 1.4426950408889634
HIGH = lax.Precision.HIGHEST
V = pl.BlockSpec(memory_space=pltpu.VMEM)

def index_maps():
    pw1 = np.zeros((512, 448), np.float32)
    pw2 = np.zeros((512, 192), np.float32)
    ps = np.zeros((192, 448), np.float32)
    for s in range(2):
        for i in range(14):
            for j in range(14):
                w = (s * 2 + i // 7) * 2 + j // 7
                t = 64 * w + (i % 7) * 7 + j % 7
                flat = lambda a, b: (s * 14 + a) * 16 + b
                if i < 11 and j < 11:
                    pw1[t, flat(i + 3, j + 3)] = 1
                    continue
                if i >= 11 and j < 11:
                    slot, src = s * 33 + (i - 11) * 11 + j, flat(i - 11, j + 3)
                elif i < 11:
                    slot, src = 80 + s * 33 + i * 3 + j - 11, flat(i + 3, j - 11)
                else:
                    slot, src = 160 + s * 9 + (i - 11) * 3 + j - 11, flat(i - 11, j - 11)
                pw2[t, slot] = 1
                ps[slot, src] = 1
    ea = np.zeros((2, 128, 128), np.float32)
    eb = np.zeros((56, 96), np.float32)
    er = np.zeros((96, 56), np.float32)
    for a in range(49):
        off = (a // 7) * 13 + a % 7
        ea[0, off, a] = 1
        ea[1, off, 64 + a] = 1
        eb[a, off] = 1
        er[92 - off, a] = 1
    hm = (np.arange(256)[:, None] // 64 == np.arange(128)[None, :] // 32).astype(np.float32)
    return pw1, pw2, ps, ea, eb, er, hm

def fill_flat(flat, x, u):
    flat[...] = jnp.zeros_like(flat)
    for s in range(2):
        for i in range(14):
            k = 16 * (s * 14 + i)
            flat[k:k + 14, 0:384] = x[s, i]
            flat[k:k + 14, 384:768] = u[s, i]

def dot(a, b, ca=1, cb=0, **kw):
    return lax.dot_general(a, b, (((ca,), (cb,)), ((), ())), preferred_element_type=f32, **kw)

def halo_kernel(x, u, ps, out, flat, box, ss, rs):
    row, z, scene = lax.axis_index("row"), lax.axis_index("col"), lax.axis_index("scene")
    rm, zm = lax.rem(row + 7, 8), lax.rem(z + 7, 8)
    rp, zp = lax.rem(row + 1, 8), lax.rem(z + 1, 8)
    bar = pltpu.get_barrier_semaphore()
    for d in ((rp, z, scene), (row, zp, scene), (rp, zp, scene)):
        pl.semaphore_signal(bar, inc=1, device_id=d, device_id_type=MESH)
    fill_flat(flat, x, u)
    box[...] = dot(ps[...], flat[...]).astype(bf16)
    pl.semaphore_wait(bar, 3)
    copies = []
    for i, (d, lo, n) in enumerate((((rm, z, scene), 0, 80), ((row, zm, scene), 80, 80), ((rm, zm, scene), 160, 32))):
        c = pltpu.make_async_remote_copy(src_ref=box.at[pl.ds(lo, n)], dst_ref=out.at[pl.ds(lo, n)], send_sem=ss.at[i],
                                         recv_sem=rs.at[i], device_id=d, device_id_type=MESH)
        c.start()
        copies.append(c)
    for c in copies:
        c.wait()

def halo(x, u, ps):
    return pl.pallas_call(
        halo_kernel, out_shape=jax.ShapeDtypeStruct((192, 768), bf16), in_specs=[V] * 3, out_specs=V,
        scratch_shapes=[pltpu.VMEM((448, 768), bf16), pltpu.VMEM((192, 768), bf16), pltpu.SemaphoreType.DMA((3,)), pltpu.SemaphoreType.DMA((3,))],
        compiler_params=pltpu.CompilerParams(collective_id=0, has_side_effects=True, vmem_limit_bytes=48 << 20),
    )(x, u, ps)

def bias_tables(table, ea, eb, tbl, wide):
    tt = tbl[...]
    tt[...] if False else None

def local_kernel(where, x, u, rx, gain, shift, wqkv, bqkv, wproj, table, pw1, pw2, q1, q2, ea, eb, er, hm,
                 g_out, gl_out, hs_out,
                 flat, xhat, norm, up, qkv, gat, attn, gq, tvar, gtab, tab, small, gsh):
    row, col = where()
    tab[...] = jnp.zeros_like(tab)
    tab[4:173, 0:12] = table[...] * LOG2E
    heads = tab[...].T
    for pair in range(6):
        acc = None
        for half in range(2):
            h = 2 * pair + half
            wide = jnp.broadcast_to(heads[h:h + 1], (96, 256))
            wide = pltpu.roll(wide, 168, 1, stride=1, stride_axis=0)[:, :128]
            rows = dot(eb[...], wide, precision=HIGH)
            part = dot(rows, ea[half], precision=HIGH)
            acc = part if acc is None else acc + part
        tvar[0, pair // 2, :, (pair % 2) * 128:(pair % 2) * 128 + 128] = acc
    key = lax.broadcasted_iota(jnp.int32, (56, 256), 0)
    query = lax.broadcasted_iota(jnp.int32, (56, 256), 1) & 63
    def low(t):
        return ((t >= 28).astype(jnp.int32), ((t - 7 * ((t * 37) >> 8)) >= 4).astype(jnp.int32))
    (ky, kx), (qy, qx) = low(key), low(query)
    pad = key >= 49
    bad_row = ((ky != qy) & (query < 49)) & (row == 7)
    bad_col = ((kx != qx) & (query < 49)) & (col == 7)
    for grp in range(3):
        t = jnp.where(pad, MASKED, tvar[0, grp])
        tvar[0, grp] = t
        tr = jnp.where(bad_row, MASKED, t)
        tvar[1, grp] = jnp.where(bad_col, MASKED, t)
        tvar[2, grp] = tr
        tvar[3, grp] = jnp.where(bad_col, MASKED, tr)

    fill_flat(flat, x, u)
    for half in range(2):
        lanes = slice(384 * half, 384 * half + 384)
        v = dot(pw1[...], flat[:, lanes]) + dot(pw2[...], rx[:, lanes])
        if half:
            up[...] = v.astype(bf16)
        else:
            mean = jnp.sum(v, axis=1, keepdims=True) * (1.0 / 384)
            c = v - mean
            var = jnp.sum(c * c, axis=1, keepdims=True) * (1.0 / 384)
            rstd = lax.rsqrt(var + NORM_EPS)
            xh = c * rstd
            xhat[...] = xh
            norm[...] = (xh * gain[...] + shift[...]).astype(bf16)
    for n in range(3):
        lanes = slice(384 * n, 384 * n + 384)
        qkv[:, lanes] = (dot(norm[...], wqkv[:, lanes]) + bqkv[:, lanes]).astype(bf16)
    gat[...] = dot(up[...], wproj[...], 1, 1).astype(bf16)
    gtab[...] = jnp.zeros_like(gtab)
    gq[...] = jnp.zeros_like(gq)
    scale = 32 ** -0.5
    lane = lax.broadcasted_iota(jnp.int32, (64, 128), 1)
    def merge(r):
        return jnp.where(lane < 32, r[0:64], jnp.where(lane < 64, r[64:128], jnp.where(lane < 96, r[128:192], r[192:256])))
    def window(w, carry):
        base = pl.multiple_of(w * 64, 64)
        var = lax.rem(w, 4)
        for grp in range(3):
            at_ = lambda n: slice(384 * n + 128 * grp, 384 * n + 128 * grp + 128)
            q = qkv[pl.ds(base, 64), at_(0)]
            k = qkv[pl.ds(base, 56), at_(1)]
            vv = qkv[pl.ds(base, 56), at_(2)]
            ga = gat[pl.ds(base, 64), at_(0)]
            qx = jnp.concatenate([q, q, q, q], axis=0) * hm[...]
            gx = jnp.concatenate([ga, ga, ga, ga], axis=0) * hm[...]
            s = dot(k, qx, 1, 1) * (scale * LOG2E) + tvar[var, grp]
            e = jnp.exp2(s - jnp.max(s, axis=0, keepdims=True))
            p = e * (1.0 / jnp.sum(e, axis=0, keepdims=True))
            pb = p.astype(bf16)
            attn[pl.ds(base, 64), at_(0)] = merge(dot(pb, vv, 0, 0)).astype(bf16)
            dp = dot(vv, gx, 1, 1)
            ds = p * (dp - jnp.sum(dp * p, axis=0, keepdims=True))
            gtab[grp] += ds
            db = ds.astype(bf16)
            gq[pl.ds(base, 64), at_(0)] = (merge(dot(db, k, 0, 0)) * scale).astype(bf16)
            gq[pl.ds(base, 56), at_(1)] = (dot(db, qx) * scale).astype(bf16)
            gq[pl.ds(base, 56), at_(2)] = dot(pb, gx).astype(bf16)
        return carry
    lax.fori_loop(0, 8, window, 0)

    def put(lb, m):
        for i in range(24):
            t = lb * 24 + i
            g_out[t // 9, t % 9] = m[16 * i:16 * i + 16].astype(bf16)
    for n in range(3):
        m = dot(attn[...], up[:, 128 * n:128 * n + 128], 0, 0)
        put(9 + n, m)
    for n in range(9):
        put(n, dot(norm[...], gq[:, 128 * n:128 * n + 128], 0, 0))
    ones = jnp.ones((16, 512), bf16)
    sq = dot(ones, gq[...])[0:1]
    sp = dot(ones, up[...])[0:1]
    for n in range(9):
        small[6 + n:7 + n] = sq[:, 128 * n:128 * n + 128]
    for n in range(3):
        small[15 + n:16 + n] = sp[:, 128 * n:128 * n + 128]
    for pair in range(6):
        d = gtab[pair // 2, :, (pair % 2) * 128:(pair % 2) * 128 + 128]
        for half in range(2):
            h = 2 * pair + half
            wide = dot(er[...], dot(d, ea[half], 1, 1, precision=HIGH), precision=HIGH)
            wide = jnp.concatenate([wide, jnp.zeros_like(wide)], axis=1)
            wide = pltpu.roll(wide, 248, 1, stride=1, stride_axis=0)
            u_h = jnp.sum(wide, axis=0, keepdims=True)
            small[18 + 2 * h:19 + 2 * h] = u_h[:, :128]
            small[19 + 2 * h:20 + 2 * h] = u_h[:, 128:]
    gn = dot(gq[...], wqkv[...], 1, 1).astype(bf16).astype(f32)
    xh = xhat[...]
    a = jnp.sum(gn * xh, axis=0, keepdims=True)
    b = jnp.sum(gn, axis=0, keepdims=True)
    for n in range(3):
        small[n:n + 1] = a[:, 128 * n:128 * n + 128]
        small[3 + n:4 + n] = b[:, 128 * n:128 * n + 128]
    small[42:48] = jnp.zeros((6, 128), f32)
    for c in range(32):
        if c < 6:
            t = small[8 * c:8 * c + 8]
            hi = t.astype(bf16).astype(f32)
            g_out[c, 9] = jnp.concatenate([hi, t - hi], axis=0).astype(bf16)
        else:
            g_out[c, 9] = jnp.zeros((16, 128), bf16)
    gg = gn * gain[...]
    m1 = jnp.sum(gg, axis=1, keepdims=True) * (1.0 / 384)
    m2 = jnp.sum(gg * xh, axis=1, keepdims=True) * (1.0 / 384)
    v = dot(pw1[...], flat[:, 0:384]) + dot(pw2[...], rx[:, 0:384])
    c = v - jnp.sum(v, axis=1, keepdims=True) * (1.0 / 384)
    rstd = lax.rsqrt(jnp.sum(c * c, axis=1, keepdims=True) * (1.0 / 384) + NORM_EPS)
    gsh[...] = ((gg - m1 - xh * m2) * rstd).astype(bf16)
    gl_out[...] = dot(q1[...], gsh[...]).astype(bf16)
    hs_out[...] = dot(q2[...], gsh[...]).astype(bf16)

def here():
    return lax.axis_index("row"), lax.axis_index("col")

def local(x, u, rx, gain, shift, wqkv, bqkv, wproj, table, maps, where=here):
    pw1, pw2, ps, ea, eb, er, hm = maps
    c = lambda a: jnp.asarray(a, bf16)
    S = pltpu.VMEM
    return pl.pallas_call(
        functools.partial(local_kernel, where),
        out_shape=(jax.ShapeDtypeStruct((32, 10, 16, 128), bf16), jax.ShapeDtypeStruct((448, 384), bf16), jax.ShapeDtypeStruct((192, 384), bf16)),
        in_specs=[V] * 17, out_specs=(V, V, V),
        scratch_shapes=[S((448, 768), bf16), S((512, 384), f32), S((512, 384), bf16), S((512, 384), bf16), S((512, 1152), bf16),
                        S((512, 384), bf16), S((512, 384), bf16), S((512, 1152), bf16), S((4, 3, 56, 256), f32), S((3, 56, 256), f32),
                        S((256, 128), f32), S((48, 128), f32), S((512, 384), bf16)],
        compiler_params=pltpu.CompilerParams(vmem_limit_bytes=56 << 20),
    )(x, u, rx, gain.reshape(1, -1), shift.reshape(1, -1), wqkv, bqkv.reshape(1, -1), wproj, table,
      c(pw1), c(pw2), c(pw1.T), c(pw2.T), jnp.asarray(ea), jnp.asarray(eb), jnp.asarray(er), c(hm))

def final_kernel(scale, g, u, gl, hr, q3, gx_out, a_out, b_out, wq_out, bq_out, wp_out, bp_out, t_out, small, tab):
    got = gl[...].astype(f32) + dot(q3[...], hr[...])
    for s in range(2):
        for i in range(14):
            k = 16 * (s * 14 + i)
            gx_out[s, i] = (u[s, i].astype(f32) + got[k:k + 14]).astype(bf16)
    for lb in range(12):
        dst, l = (wq_out, lb) if lb < 9 else (wp_out, lb - 9)
        for i in range(24):
            t = lb * 24 + i
            dst[16 * i:16 * i + 16, 128 * l:128 * l + 128] = g[t // 9, t % 9].astype(f32) * scale
    for c in range(6):
        t = g[c, 9].astype(f32)
        small[8 * c:8 * c + 8] = (t[:8] + t[8:]) * scale
    for n in range(3):
        a_out[:, 128 * n:128 * n + 128] = small[n:n + 1]
        b_out[:, 128 * n:128 * n + 128] = small[3 + n:4 + n]
        bp_out[:, 128 * n:128 * n + 128] = small[15 + n:16 + n]
    for n in range(9):
        bq_out[:, 128 * n:128 * n + 128] = small[6 + n:7 + n]
    tab[...] = jnp.zeros_like(tab)
    for h in range(12):
        tab[h:h + 1, 0:128] = small[18 + 2 * h:19 + 2 * h]
        tab[h:h + 1, 128:256] = small[19 + 2 * h:20 + 2 * h]
    t_out[...] = tab[...].T[0:169, 0:12]

def final(scale, g, u, gl, hr, maps):
    s = jax.ShapeDtypeStruct
    o = pl.pallas_call(
        functools.partial(final_kernel, scale),
        out_shape=(s((2, 14, 14, 384), bf16), s((1, 384), f32), s((1, 384), f32), s((384, 1152), f32), s((1, 1152), f32), s((384, 384), f32), s((1, 384), f32), s((169, 12), f32)),
        in_specs=[V] * 5, out_specs=(V,) * 8,
        scratch_shapes=[pltpu.VMEM((48, 128), f32), pltpu.VMEM((128, 256), f32)],
        compiler_params=pltpu.CompilerParams(vmem_limit_bytes=48 << 20),
    )(g, u, gl, hr, jnp.asarray(maps[2].T, bf16))
    return o

def on_device(features, grad_out, norm_gain, norm_shift, qkv_weight, qkv_bias, proj_weight, bias_table):
    maps = index_maps()
    rx = halo(features, grad_out, jnp.asarray(maps[2], bf16))
    g, gl, hs = local(features, grad_out, rx, norm_gain, norm_shift, qkv_weight, qkv_bias, proj_weight, bias_table, maps)
    g, hr = reduce_all(g, hs)
    scale = 1.0 / math.sqrt(8 * 112 * 112)
    gx, a, b, wq, bq, wp, bp, t = final(scale, g, grad_out, gl, hr, maps)
    return gx, a.reshape(-1), b.reshape(-1), wq, bq.reshape(-1), wp, bp.reshape(-1), t


def solution(mesh):
    return jax.shard_map(
        on_device,
        mesh=mesh,
        in_specs=(P("scene", "row", "col", None),) * 2 + (P(),) * 6,
        out_specs=(P("scene", "row", "col", None),) + (P(),) * 7,
        check_vma=False,
    )
```

```python
import functools
import math

import jax
import jax.numpy as jnp
import numpy as np
from jax import lax
from jax.experimental import pallas as pl
from jax.experimental.pallas import tpu as pltpu
from jax.sharding import PartitionSpec as P

WIN, SHIFT, NORM_EPS, MASKED = 7, 3, 1e-05, -1e30
LOG2E = 1.4426950408889634
HIGH = lax.Precision.HIGHEST
MESH = pl.DeviceIdType.MESH
f32, bf16 = jnp.float32, jnp.bfloat16
V = pl.BlockSpec(memory_space=pltpu.VMEM)


def index_maps():
    pw1 = np.zeros((512, 392), np.float32)
    pw2 = np.zeros((512, 192), np.float32)
    ps = np.zeros((192, 392), np.float32)
    for s in range(2):
        for i in range(14):
            for j in range(14):
                w = (s * 2 + i // 7) * 2 + j // 7
                t = 64 * w + (i % 7) * 7 + j % 7
                flat = lambda a, b: (a * 14 + b) * 2 + s
                if i < 11 and j < 11:
                    pw1[t, flat(i + 3, j + 3)] = 1
                    continue
                if i >= 11 and j < 11:
                    slot, src = s * 33 + (i - 11) * 11 + j, flat(i - 11, j + 3)
                elif i < 11:
                    slot, src = 80 + s * 33 + i * 3 + j - 11, flat(i + 3, j - 11)
                else:
                    slot, src = 160 + s * 9 + (i - 11) * 3 + j - 11, flat(i - 11, j - 11)
                pw2[t, slot] = 1
                ps[slot, src] = 1
    ea = np.zeros((2, 128, 128), np.float32)
    eb = np.zeros((56, 96), np.float32)
    er = np.zeros((96, 56), np.float32)
    for a in range(49):
        off = (a // 7) * 13 + a % 7
        ea[0, off, a] = 1
        ea[1, off, 64 + a] = 1
        eb[a, off] = 1
        er[92 - off, a] = 1
    hm = (np.arange(256)[:, None] // 64 == np.arange(128)[None, :] // 32).astype(np.float32)
    return pw1, pw2, ps, ea, eb, er, hm


def place():
    row, z, scene = lax.axis_index("row"), lax.axis_index("col"), lax.axis_index("scene")
    x = (row // 4) * 2 + scene // 2
    return x, row % 4, z, scene % 2


def at(x, y, z, core):
    return ((x // 2) * 4 + y, z, (x % 2) * 2 + core)


def dot(a, b, ca=1, cb=0, **kw):
    return lax.dot_general(a, b, (((ca,), (cb,)), ((), ())), preferred_element_type=f32, **kw)


def split(t):
    hi = t.astype(bf16).astype(f32)
    return jnp.concatenate([hi, t - hi], axis=0).astype(bf16)


def main_kernel(
    x, u, gain, shift, wqkv, bqkv, wproj, table, pw1, pw2, ps, q1, q2, ea, eb, er, hm,
    out, gl, hout,
    flat, box, rx, xhat, rstd, norm, up, qkv, gat, attn, gq, tvar, gtab, tab, small, gsh,
    g, r0, s1, r1, acc, sg, t0, ts, t1, tacc, s2, r2, hbox,
    hs, hr, bs, br, p0s, p0r, p1s, p1r, q0s, q0r, q1s, q1r, p2s, p2r, p3s, p3r, p4s, p4r, p5s, p5r,
):
    px, py, z, core = place()
    me = px * 4 + py
    row, scene = lax.axis_index("row"), lax.axis_index("scene")
    rm, zm = lax.rem(row + 7, 8), lax.rem(z + 7, 8)
    rp, zp = lax.rem(row + 1, 8), lax.rem(z + 1, 8)
    sib = at(px, py, z, 1 - core)

    def plane(k):
        return at(lax.rem(px + k // 4, 4), lax.rem(py + k % 4, 4), z, core)

    def plane_from(k):
        return lax.rem(px + 4 - k // 4, 4) * 4 + lax.rem(py + 4 - k % 4, 4)

    def depth(k):
        return at(px, py, lax.rem(z + k, 8), core)

    def send(src, dst, ss, rs, dev):
        return pltpu.make_async_remote_copy(
            src_ref=src, dst_ref=dst, send_sem=ss, recv_sem=rs, device_id=dev, device_id_type=MESH
        )

    bar = pltpu.get_barrier_semaphore()
    peers = [sib] + [plane(k) for k in range(1, 16)] + [depth(k) for k in range(1, 8)]
    peers += [(rm, zm, scene), (rp, zp, scene)]
    for d in peers:
        pl.semaphore_signal(bar, inc=1, device_id=d, device_id_type=MESH)

    for p in range(196):
        flat[2 * p : 2 * p + 2, 0:384] = x[p]
        flat[2 * p : 2 * p + 2, 384:768] = u[p]
    box[...] = dot(ps[...], flat[...]).astype(bf16)
    pl.semaphore_wait(bar, len(peers))
    pieces = ((0, 80), (80, 80), (160, 32))
    halo = []
    for i, (d, (lo, n)) in enumerate(zip(((rm, z, scene), (row, zm, scene), (rm, zm, scene)), pieces)):
        c = send(box.at[pl.ds(lo, n)], rx.at[pl.ds(lo, n)], hs.at[i], hr.at[i], d)
        c.start()
        halo.append(c)

    tab[...] = jnp.zeros_like(tab)
    tab[0:12, 0:169] = table[...] * LOG2E
    heads = pltpu.roll(tab[...], 4, 1)
    for pair in range(6):
        parts = []
        for half in range(2):
            h = 2 * pair + half
            wide = jnp.broadcast_to(heads[h : h + 1], (96, 256))
            wide = pltpu.roll(wide, 168, 1, stride=1, stride_axis=0)[:, :128]
            rows = dot(eb[...], wide, precision=HIGH)
            parts.append(dot(rows, ea[half], precision=HIGH))
        lo = (pair % 2) * 128
        tvar[0, pair // 2, :, lo : lo + 128] = parts[0] + parts[1]
    key = lax.broadcasted_iota(jnp.int32, (56, 256), 0)
    query = lax.broadcasted_iota(jnp.int32, (56, 256), 1) & 63

    def low(t):
        return (t >= 28).astype(jnp.int32), ((t - 7 * ((t * 37) >> 8)) >= 4).astype(jnp.int32)

    (ky, kx), (qy, qx_) = low(key), low(query)
    pad = key >= 49
    bad_row = ((ky != qy) & (query < 49)) & (row == 7)
    bad_col = ((kx != qx_) & (query < 49)) & (z == 7)
    for grp in range(3):
        t = jnp.where(pad, MASKED, tvar[0, grp])
        tvar[0, grp] = t
        tr = jnp.where(bad_row, MASKED, t)
        tvar[1, grp] = jnp.where(bad_col, MASKED, t)
        tvar[2, grp] = tr
        tvar[3, grp] = jnp.where(bad_col, MASKED, tr)
    gtab[...] = jnp.zeros_like(gtab)
    gq[...] = jnp.zeros_like(gq)

    for c in halo:
        c.wait_recv()
    v = dot(pw1[...], flat[:, 384:768]) + dot(pw2[...], rx[:, 384:768])
    up[...] = v.astype(bf16)
    v = dot(pw1[...], flat[:, 0:384]) + dot(pw2[...], rx[:, 0:384])
    cen = v - jnp.sum(v, axis=1, keepdims=True) * (1.0 / 384)
    inv = lax.rsqrt(jnp.sum(cen * cen, axis=1, keepdims=True) * (1.0 / 384) + NORM_EPS)
    rstd[...] = inv
    xh = cen * inv
    xhat[...] = xh
    norm[...] = (xh * gain[...].reshape(1, 384) + shift[...].reshape(1, 384)).astype(bf16)
    for n in range(3):
        lanes = slice(384 * n, 384 * n + 384)
        qkv[:, lanes] = (dot(norm[...], wqkv[:, lanes]) + bqkv[...].reshape(1, 1152)[:, lanes]).astype(bf16)
    gat[...] = dot(up[...], wproj[...], 1, 1).astype(bf16)

    scale = 32**-0.5
    lane = lax.broadcasted_iota(jnp.int32, (64, 128), 1)

    def merge(r):
        return jnp.where(
            lane < 32, r[0:64], jnp.where(lane < 64, r[64:128], jnp.where(lane < 96, r[128:192], r[192:256]))
        )

    def window(w, carry):
        base = pl.multiple_of(w * 64, 64)
        var = lax.rem(w, 4)
        for grp in range(3):
            lanes = [slice(384 * n + 128 * grp, 384 * n + 128 * grp + 128) for n in range(3)]
            q = qkv[pl.ds(base, 64), lanes[0]]
            k = qkv[pl.ds(base, 56), lanes[1]]
            vv = qkv[pl.ds(base, 56), lanes[2]]
            ga = gat[pl.ds(base, 64), lanes[0]]
            qx = jnp.concatenate([q, q, q, q], axis=0) * hm[...]
            gx = jnp.concatenate([ga, ga, ga, ga], axis=0) * hm[...]
            s = dot(k, qx, 1, 1) * (scale * LOG2E) + tvar[var, grp]
            e = jnp.exp2(s - jnp.max(s, axis=0, keepdims=True))
            p = e * (1.0 / jnp.sum(e, axis=0, keepdims=True))
            pb = p.astype(bf16)
            attn[pl.ds(base, 64), lanes[0]] = merge(dot(pb, vv, 0, 0)).astype(bf16)
            dp = dot(vv, gx, 1, 1)
            ds = p * (dp - jnp.sum(dp * p, axis=0, keepdims=True))
            gtab[grp] += ds
            db = ds.astype(bf16)
            gq[pl.ds(base, 64), lanes[0]] = (merge(dot(db, k, 0, 0)) * scale).astype(bf16)
            gq[pl.ds(base, 56), lanes[1]] = (dot(db, qx) * scale).astype(bf16)
            gq[pl.ds(base, 56), lanes[2]] = dot(pb, gx).astype(bf16)
        return carry

    lax.fori_loop(0, 8, window, 0)

    def put(lb, m):
        for i in range(24):
            t = lb * 24 + i
            g[t // 9, t % 9] = m[16 * i : 16 * i + 16].astype(bf16)

    for n in range(3):
        m = dot(attn[...], up[:, 128 * n : 128 * n + 128], 0, 0)
        put(9 + n, m)
    for n in range(9):
        put(n, dot(norm[...], gq[:, 128 * n : 128 * n + 128], 0, 0))

    def chunk(k):
        return lax.rem(px + k // 4, 4) * 4 + lax.rem(py + k % 4, 4)

    order = list(range(1, 16)) + [0]
    c0, c1 = [None] * 16, [None] * 16
    for k in order:
        c = chunk(k)
        c0[k] = send(g.at[(1 - core) * 16 + c], r0.at[c], p0s.at[k], p0r.at[k], sib)
        c0[k].start()

    gn = dot(gq[...], wqkv[...], 1, 1).astype(bf16).astype(f32)
    xh = xhat[...]
    a = jnp.sum(gn * xh, axis=0, keepdims=True)
    b = jnp.sum(gn, axis=0, keepdims=True)
    for n in range(3):
        small[n : n + 1] = a[:, 128 * n : 128 * n + 128]
        small[3 + n : 4 + n] = b[:, 128 * n : 128 * n + 128]

    for k in order:
        c = chunk(k)
        c0[k].wait_recv()
        total = g[core * 16 + c].astype(f32) + r0[c].astype(f32)
        if k:
            s1[c] = total.astype(bf16)
            c1[k] = send(s1.at[c], r1.at[k], p1s.at[k], p1r.at[k], plane(k))
            c1[k].start()
        else:
            acc[...] = total

    gg = gn * gain[...].reshape(1, 384)
    m1 = jnp.sum(gg, axis=1, keepdims=True) * (1.0 / 384)
    m2 = jnp.sum(gg * xh, axis=1, keepdims=True) * (1.0 / 384)
    gsh[...] = ((gg - m1 - xh * m2) * rstd[...]).astype(bf16)
    hbox[...] = dot(q2[...], gsh[...]).astype(bf16)
    back = []
    for i, (d, (lo, n)) in enumerate(zip(((rp, z, scene), (row, zp, scene), (rp, zp, scene)), pieces)):
        c = send(hbox.at[pl.ds(lo, n)], hout.at[pl.ds(lo, n)], bs.at[i], br.at[i], d)
        c.start()
        back.append(c)
    gl[...] = dot(q1[...], gsh[...]).astype(bf16)

    ones = jnp.ones((16, 512), bf16)
    sq = dot(ones, gq[...])[0:1]
    sp = dot(ones, up[...])[0:1]
    for n in range(9):
        small[6 + n : 7 + n] = sq[:, 128 * n : 128 * n + 128]
    for n in range(3):
        small[15 + n : 16 + n] = sp[:, 128 * n : 128 * n + 128]
    for pair in range(6):
        lo = (pair % 2) * 128
        d = gtab[pair // 2, :, lo : lo + 128]
        for half in range(2):
            h = 2 * pair + half
            wide = dot(er[...], dot(d, ea[half], 1, 1, precision=HIGH), precision=HIGH)
            wide = jnp.concatenate([wide, jnp.zeros_like(wide)], axis=1)
            wide = pltpu.roll(wide, 248, 1, stride=1, stride_axis=0)
            u_h = jnp.sum(wide, axis=0, keepdims=True)
            small[18 + 2 * h : 19 + 2 * h] = u_h[:, :128]
            small[19 + 2 * h : 20 + 2 * h] = u_h[:, 128:]
    small[42:48] = jnp.zeros((6, 128), f32)
    for c in range(32):
        sg[c] = split(small[8 * c : 8 * c + 8]) if c < 6 else jnp.zeros((16, 128), bf16)
    d0 = send(sg.at[pl.ds((1 - core) * 16, 16)], t0, q0s, q0r, sib)
    d0.start()
    d0.wait_recv()
    d1 = [None] * 16
    for k in order:
        c = chunk(k)
        total = sg[core * 16 + c].astype(f32) + t0[c].astype(f32)
        total = total[:8] + total[8:]
        if k:
            ts[c] = split(total)
            d1[k] = send(ts.at[c], t1.at[k], q1s.at[k], q1r.at[k], plane(k))
            d1[k].start()
        else:
            tacc[...] = total

    for k in range(1, 16):
        c1[k].wait_recv()
        acc[...] += r1[k].astype(f32)
    for k in range(1, 16):
        d1[k].wait_recv()
        t = t1[k].astype(f32)
        tacc[...] += t[:8] + t[8:]

    big, little = acc[...].astype(bf16), split(tacc[...])
    for t in range(8):
        s2[t, 0] = big[t]
        s2[t, 1] = big[8]
        s2[t, 2] = little
    c2, c3, c4, c5 = [None] * 8, [None] * 8, [None] * 16, [None] * 16
    for k in range(1, 8):
        d = lax.rem(z + k, 8)
        c2[k] = send(s2.at[d], r2.at[z], p2s.at[k], p2r.at[k], depth(k))
        c2[k].start()
    r2[z] = s2[z]
    for k in range(1, 8):
        fr = lax.rem(z + 8 - k, 8)
        send(s2.at[fr], r2.at[fr], p2s.at[k], p2r.at[k], depth(k)).wait_recv()
    t3 = r2[0].astype(f32)
    for t in range(1, 8):
        t3 += r2[t].astype(f32)
    mine = core * 16 + me
    out[mine, z] = t3[0].astype(bf16)
    for k in range(1, 8):
        c3[k] = send(out.at[mine, z], out.at[mine, z], p3s.at[k], p3r.at[k], depth(k))
        c3[k].start()
    out[mine, 8] = t3[1].astype(bf16)
    out[mine, 9] = split(t3[2, :8] + t3[2, 8:])
    for k in range(1, 8):
        fr = lax.rem(z + 8 - k, 8)
        send(out.at[mine, fr], out.at[mine, fr], p3s.at[k], p3r.at[k], depth(k)).wait_recv()
    for k in range(1, 16):
        c4[k] = send(out.at[mine], out.at[mine], p4s.at[k], p4r.at[k], plane(k))
        c4[k].start()
    c5[0] = send(out.at[mine], out.at[mine], p5s.at[0], p5r.at[0], sib)
    c5[0].start()
    for k in range(1, 16):
        f = core * 16 + plane_from(k)
        send(out.at[f], out.at[f], p4s.at[k], p4r.at[k], plane(k)).wait_recv()
        c5[k] = send(out.at[f], out.at[f], p5s.at[k], p5r.at[k], sib)
        c5[k].start()
    for k in range(16):
        f = (1 - core) * 16 + plane_from(k)
        send(out.at[f], out.at[f], p5s.at[k], p5r.at[k], sib).wait_recv()
    for c in back:
        c.wait_recv()
    for c in halo + back + c0 + c1 + [d0] + d1 + c2 + c3 + c4 + c5:
        if c is not None:
            c.wait_send()


def run_main(x, u, gain, shift, wqkv, bqkv, wproj, table, maps):
    pw1, pw2, ps, ea, eb, er, hm = maps
    c = lambda a: jnp.asarray(a, bf16)
    S, s, D = pltpu.VMEM, jax.ShapeDtypeStruct, pltpu.SemaphoreType.DMA
    sems = [D((n,)) for n in (3, 3, 3, 3, 16, 16, 16, 16)] + [D(()), D(())]
    sems += [D((n,)) for n in (16, 16, 8, 8, 8, 8, 16, 16, 16, 16)]
    return pl.pallas_call(
        main_kernel,
        out_shape=(s((32, 10, 16, 128), bf16), s((392, 384), bf16), s((192, 384), bf16)),
        in_specs=[V] * 17,
        out_specs=(V, V, V),
        scratch_shapes=[
            S((392, 768), bf16), S((192, 768), bf16), S((192, 768), bf16),
            S((512, 384), f32), S((512, 1), f32), S((512, 384), bf16), S((512, 384), bf16),
            S((512, 1152), bf16), S((512, 384), bf16), S((512, 384), bf16), S((512, 1152), bf16),
            S((4, 3, 56, 256), f32), S((3, 56, 256), f32), S((16, 256), f32), S((48, 128), f32), S((512, 384), bf16),
            S((32, 9, 16, 128), bf16), S((16, 9, 16, 128), bf16), S((16, 9, 16, 128), bf16), S((16, 9, 16, 128), bf16),
            S((9, 16, 128), f32), S((32, 16, 128), bf16), S((16, 16, 128), bf16), S((16, 16, 128), bf16),
            S((16, 16, 128), bf16), S((8, 128), f32), S((8, 3, 16, 128), bf16), S((8, 3, 16, 128), bf16),
            S((192, 384), bf16),
        ] + sems,
        compiler_params=pltpu.CompilerParams(collective_id=0, has_side_effects=True, vmem_limit_bytes=50 << 20),
    )(x, u, gain, shift, wqkv, bqkv, wproj, table, c(pw1), c(pw2), c(ps), c(pw1.T), c(pw2.T),
      jnp.asarray(ea), jnp.asarray(eb), jnp.asarray(er), c(hm))


def final_kernel(scale, g, u, gl, hr, q3, gx_out, a_out, b_out, wq_out, bq_out, wp_out, bp_out, t_out, small, tab):
    got = gl[...].astype(f32) + dot(q3[...], hr[...])
    for p in range(196):
        gx_out[p] = (u[p].astype(f32) + got[2 * p : 2 * p + 2]).astype(bf16)
    for lb in range(12):
        dst, l = (wq_out, lb) if lb < 9 else (wp_out, lb - 9)
        for i in range(24):
            t = lb * 24 + i
            dst[16 * i : 16 * i + 16, 128 * l : 128 * l + 128] = g[t // 9, t % 9].astype(f32) * scale
    for c in range(6):
        t = g[c, 9].astype(f32)
        small[8 * c : 8 * c + 8] = (t[:8] + t[8:]) * scale
    for n in range(3):
        d = pl.ds(128 * n, 128)
        a_out[d] = small[n]
        b_out[d] = small[3 + n]
        bp_out[d] = small[15 + n]
    for n in range(9):
        bq_out[pl.ds(128 * n, 128)] = small[6 + n]
    tab[...] = jnp.zeros_like(tab)
    for h in range(12):
        tab[h : h + 1, 0:128] = small[18 + 2 * h : 19 + 2 * h]
        tab[h : h + 1, 128:256] = small[19 + 2 * h : 20 + 2 * h]
    t_out[...] = tab[0:12, 0:169]


def run_final(scale, g, u, gl, hr, maps):
    s = jax.ShapeDtypeStruct
    return pl.pallas_call(
        functools.partial(final_kernel, scale),
        out_shape=(
            s((196, 2, 384), bf16), s((384,), f32), s((384,), f32), s((384, 1152), f32),
            s((1152,), f32), s((384, 384), f32), s((384,), f32), s((12, 169), f32),
        ),
        in_specs=[V] * 5,
        out_specs=(V,) * 8,
        scratch_shapes=[pltpu.VMEM((48, 128), f32), pltpu.VMEM((16, 256), f32)],
        compiler_params=pltpu.CompilerParams(vmem_limit_bytes=40 << 20),
    )(g, u, gl, hr, jnp.asarray(maps[2].T, bf16))


def on_device(features, grad_out, norm_gain, norm_shift, qkv_weight, qkv_bias, proj_weight, bias_table):
    maps = index_maps()
    x = features.transpose(1, 2, 0, 3).reshape(196, 2, 384)
    u = grad_out.transpose(1, 2, 0, 3).reshape(196, 2, 384)
    g, gl, hr = run_main(x, u, norm_gain, norm_shift, qkv_weight, qkv_bias, proj_weight, bias_table.T, maps)
    scale = 1.0 / math.sqrt(8 * 112 * 112)
    gx, a, b, wq, bq, wp, bp, t = run_final(scale, g, u, gl, hr, maps)
    return gx.reshape(14, 14, 2, 384).transpose(2, 0, 1, 3), a, b, wq, bq, wp, bp, t.T


def solution(mesh):
    return jax.shard_map(
        on_device,
        mesh=mesh,
        in_specs=(P("scene", "row", "col", None),) * 2 + (P(),) * 6,
        out_specs=(P("scene", "row", "col", None),) + (P(),) * 7,
        check_vma=False,
    )
```

```python
import functools
import math

import jax
import jax.numpy as jnp
import numpy as np
from jax import lax
from jax.experimental import pallas as pl
from jax.experimental.pallas import tpu as pltpu
from jax.sharding import PartitionSpec as P

WIN, SHIFT, NORM_EPS, MASKED = 7, 3, 1e-05, -1e30
LOG2E = 1.4426950408889634
UNROLL = 4
HIGH = lax.Precision.HIGHEST
MESH = pl.DeviceIdType.MESH
f32, bf16 = jnp.float32, jnp.bfloat16
V = pl.BlockSpec(memory_space=pltpu.VMEM)


def index_maps():
    pw1 = np.zeros((512, 392), np.float32)
    pw2 = np.zeros((512, 192), np.float32)
    ps = np.zeros((192, 392), np.float32)
    for s in range(2):
        for i in range(14):
            for j in range(14):
                w = (s * 2 + i // 7) * 2 + j // 7
                t = 64 * w + (i % 7) * 7 + j % 7
                flat = lambda a, b: (a * 14 + b) * 2 + s
                if i < 11 and j < 11:
                    pw1[t, flat(i + 3, j + 3)] = 1
                    continue
                if i >= 11 and j < 11:
                    slot, src = s * 33 + (i - 11) * 11 + j, flat(i - 11, j + 3)
                elif i < 11:
                    slot, src = 80 + s * 33 + i * 3 + j - 11, flat(i + 3, j - 11)
                else:
                    slot, src = 160 + s * 9 + (i - 11) * 3 + j - 11, flat(i - 11, j - 11)
                pw2[t, slot] = 1
                ps[slot, src] = 1
    ea = np.zeros((2, 128, 128), np.float32)
    eb = np.zeros((56, 96), np.float32)
    er = np.zeros((96, 56), np.float32)
    for a in range(49):
        off = (a // 7) * 13 + a % 7
        ea[0, off, a] = 1
        ea[1, off, 64 + a] = 1
        eb[a, off] = 1
        er[92 - off, a] = 1
    hm = (np.arange(256)[:, None] // 64 == np.arange(128)[None, :] // 32).astype(np.float32)
    return pw1, pw2, ps, ea, eb, er, hm


def place():
    row, z, scene = lax.axis_index("row"), lax.axis_index("col"), lax.axis_index("scene")
    x = (row // 4) * 2 + scene // 2
    return x, row % 4, z, scene % 2


def at(x, y, z, core):
    return ((x // 2) * 4 + y, z, (x % 2) * 2 + core)


def dot(a, b, ca=1, cb=0, **kw):
    return lax.dot_general(a, b, (((ca,), (cb,)), ((), ())), preferred_element_type=f32, **kw)


def split(t):
    hi = t.astype(bf16).astype(f32)
    return jnp.concatenate([hi, t - hi], axis=0).astype(bf16)


def main_kernel(
    x_in, u_in, ps_in, pw1_in, table_in, eb_in, ea_in, gain_in, shift_in, wqkv_in, bqkv_in, wproj_in, pw2_in, hm_in,
    q2_in, q1_in, er_in,
    out0, out1, out2, gl, hout,
    x, u, ps, pw1, table, eb, ea, gain, shift, wqkv, bqkv, wproj, pw2, hm, q2, q1, er, load,
    flat, box, rx, xhat, rstd, norm, up, qkv, gat, attn, gq, tvar, gtab, tab, small, gsh,
    g, r0, s1, r1_0, r1_1, r1_2, acc, sg, t0, ts, t1, tacc, s2_0, s2_1, s2_2, hbox,
    hs, hr, bs, br, p0s, p0r, p1s, p1r, q0s, q0r, q1s, q1r, p2s, p2r, p4s, p4r, p5s, p5r,
):
    px, py, z, core = place()
    me = px * 4 + py
    row, scene = lax.axis_index("row"), lax.axis_index("scene")
    rm, zm = lax.rem(row + 7, 8), lax.rem(z + 7, 8)
    rp, zp = lax.rem(row + 1, 8), lax.rem(z + 1, 8)
    sib = at(px, py, z, 1 - core)

    def plane(k):
        return at(lax.rem(px + k // 4, 4), lax.rem(py + k % 4, 4), z, core)

    def plane_from(k):
        return lax.rem(px + 4 - k // 4, 4) * 4 + lax.rem(py + 4 - k % 4, 4)

    def depth(k):
        return at(px, py, lax.rem(z + k, 8), core)

    def send(src, dst, ss, rs, dev):
        return pltpu.make_async_remote_copy(
            src_ref=src, dst_ref=dst, send_sem=ss, recv_sem=rs, device_id=dev, device_id_type=MESH
        )

    bar = pltpu.get_barrier_semaphore()
    peers = [sib] + [plane(k) for k in range(1, 16)] + [depth(k) for k in range(1, 8)]
    peers += [(rm, zm, scene), (rp, zp, scene)]
    for d in peers:
        pl.semaphore_signal(bar, inc=1, device_id=d, device_id_type=MESH)

    loads = [
        pltpu.make_async_copy(a, b, load.at[i])
        for i, (a, b) in enumerate(
            (
                (x_in, x), (u_in, u), (ps_in, ps), (pw1_in, pw1), (table_in, table), (eb_in, eb), (ea_in, ea),
                (gain_in, gain), (shift_in, shift), (wqkv_in, wqkv), (bqkv_in, bqkv), (wproj_in, wproj),
                (pw2_in, pw2), (hm_in, hm), (q2_in, q2), (q1_in, q1), (er_in, er),
            )
        )
    ]
    for c in loads:
        c.start()
    for c in loads[:3]:
        c.wait()
    for p in range(196):
        flat[2 * p : 2 * p + 2, 0:384] = x[p]
        flat[2 * p : 2 * p + 2, 384:768] = u[p]
    box[0] = dot(ps[...], flat[:, 0:384]).astype(bf16)
    box[1] = dot(ps[...], flat[:, 384:768]).astype(bf16)
    pl.semaphore_wait(bar, len(peers))
    pieces = ((0, 80), (80, 80), (160, 32))
    halo = []
    for h in range(2):
        for i, (d, (lo, n)) in enumerate(zip(((rm, z, scene), (row, zm, scene), (rm, zm, scene)), pieces)):
            i = 3 * h + i
            c = send(box.at[h, pl.ds(lo, n)], rx.at[h, pl.ds(lo, n)], hs.at[i], hr.at[i], d)
            c.start()
            halo.append(c)
    for c in loads[3:]:
        c.wait()

    tab[...] = jnp.zeros_like(tab)
    tab[0:12, 0:169] = table[...] * LOG2E
    heads = pltpu.roll(tab[...], 4, 1)
    for pair in range(6):
        parts = []
        for half in range(2):
            h = 2 * pair + half
            wide = jnp.broadcast_to(heads[h : h + 1], (96, 256))
            wide = pltpu.roll(wide, 168, 1, stride=1, stride_axis=0)[:, :128]
            rows = dot(eb[...], wide, precision=HIGH)
            parts.append(dot(rows, ea[half], precision=HIGH))
        lo = (pair % 2) * 128
        tvar[0, pair // 2, :, lo : lo + 128] = parts[0] + parts[1]
    key = lax.broadcasted_iota(jnp.int32, (56, 256), 0)
    query = lax.broadcasted_iota(jnp.int32, (56, 256), 1) & 63

    def low(t):
        return (t >= 28).astype(jnp.int32), ((t - 7 * ((t * 37) >> 8)) >= 4).astype(jnp.int32)

    (ky, kx), (qy, qx_) = low(key), low(query)
    pad = key >= 49
    bad_row = ((ky != qy) & (query < 49)) & (row == 7)
    bad_col = ((kx != qx_) & (query < 49)) & (z == 7)
    for grp in range(3):
        t = jnp.where(pad, MASKED, tvar[0, grp])
        tvar[0, grp] = t
        tr = jnp.where(bad_row, MASKED, t)
        tvar[1, grp] = jnp.where(bad_col, MASKED, t)
        tvar[2, grp] = tr
        tvar[3, grp] = jnp.where(bad_col, MASKED, tr)
    gtab[...] = jnp.zeros_like(gtab)
    gq[...] = jnp.zeros_like(gq)

    v = dot(pw1[...], flat[:, 0:384])
    for c in halo[:3]:
        c.wait_recv()
    v = v + dot(pw2[...], rx[0])
    cen = v - jnp.sum(v, axis=1, keepdims=True) * (1.0 / 384)
    inv = lax.rsqrt(jnp.sum(cen * cen, axis=1, keepdims=True) * (1.0 / 384) + NORM_EPS)
    rstd[...] = inv
    xh = cen * inv
    xhat[...] = xh
    norm[...] = (xh * gain[...].reshape(1, 384) + shift[...].reshape(1, 384)).astype(bf16)
    for n in range(3):
        lanes = slice(384 * n, 384 * n + 384)
        qkv[:, lanes] = (dot(norm[...], wqkv[:, lanes]) + bqkv[...].reshape(1, 1152)[:, lanes]).astype(bf16)
    v = dot(pw1[...], flat[:, 384:768])
    for c in halo[3:]:
        c.wait_recv()
    up[...] = (v + dot(pw2[...], rx[1])).astype(bf16)
    gat[...] = dot(up[...], wproj[...], 1, 1).astype(bf16)

    scale = 32**-0.5
    lane = lax.broadcasted_iota(jnp.int32, (64, 128), 1)

    def merge(r):
        return jnp.where(
            lane < 32, r[0:64], jnp.where(lane < 64, r[64:128], jnp.where(lane < 96, r[128:192], r[192:256]))
        )

    def window(w, carry):
        base = pl.multiple_of(w * 64, 64)
        var = lax.rem(w, 4)
        for grp in range(3):
            lanes = [slice(384 * n + 128 * grp, 384 * n + 128 * grp + 128) for n in range(3)]
            q = qkv[pl.ds(base, 64), lanes[0]]
            k = qkv[pl.ds(base, 56), lanes[1]]
            vv = qkv[pl.ds(base, 56), lanes[2]]
            ga = gat[pl.ds(base, 64), lanes[0]]
            qx = jnp.concatenate([q, q, q, q], axis=0) * hm[...]
            gx = jnp.concatenate([ga, ga, ga, ga], axis=0) * hm[...]
            s = dot(k, qx, 1, 1) * (scale * LOG2E) + tvar[var, grp]
            e = jnp.exp2(s - jnp.max(s, axis=0, keepdims=True))
            p = e * (1.0 / jnp.sum(e, axis=0, keepdims=True))
            pb = p.astype(bf16)
            attn[pl.ds(base, 64), lanes[0]] = merge(dot(pb, vv, 0, 0)).astype(bf16)
            dp = dot(vv, gx, 1, 1)
            ds = p * (dp - jnp.sum(dp * p, axis=0, keepdims=True))
            gtab[grp] += ds
            db = ds.astype(bf16)
            gq[pl.ds(base, 64), lanes[0]] = (merge(dot(db, k, 0, 0)) * scale).astype(bf16)
            gq[pl.ds(base, 56), lanes[1]] = (dot(db, qx) * scale).astype(bf16)
            gq[pl.ds(base, 56), lanes[2]] = dot(pb, gx).astype(bf16)
        return carry

    def windows(i, carry):
        for j in range(UNROLL):
            window(i * UNROLL + j, carry)
        return carry

    lax.fori_loop(0, 8 // UNROLL, windows, 0)

    out, r1, s2 = (out0, out1, out2), (r1_0, r1_1, r1_2), (s2_0, s2_1, s2_2)
    order = list(range(1, 16)) + [0]
    c0, c1, c2, c4, c5, d1 = [], [], [], [], [], [None] * 16

    def chunk(k):
        return lax.rem(px + k // 4, 4) * 4 + lax.rem(py + k % 4, 4)

    for seg in range(3):
        for n in range(4):
            lb = 4 * seg + n
            if lb < 3:
                m = dot(attn[...], up[:, 128 * lb : 128 * lb + 128], 0, 0)
            else:
                m = dot(norm[...], gq[:, 128 * (lb - 3) : 128 * (lb - 3) + 128], 0, 0)
            for i in range(24):
                t = n * 24 + i
                g[seg, t // 3, t % 3] = m[16 * i : 16 * i + 16].astype(bf16)
        c = send(g.at[seg, pl.ds((1 - core) * 16, 16)], r0.at[seg], p0s.at[seg], p0r.at[seg], sib)
        c.start()
        c0.append(c)

    def spread(seg):
        c0[seg].wait_recv()
        cs = [None] * 16
        for k in order:
            c = chunk(k)
            total = g[seg, core * 16 + c].astype(f32) + r0[seg, c].astype(f32)
            if k:
                s1[seg, c] = total.astype(bf16)
                cs[k] = send(s1.at[seg, c], r1[seg].at[k], p1s.at[seg, k], p1r.at[seg, k], plane(k))
                cs[k].start()
            else:
                acc[seg] = total
        c1.append(cs)

    def deepen(seg):
        a = acc[seg]
        for k in range(1, 16):
            c1[seg][k].wait_recv()
            a = a + r1[seg][k].astype(f32)
        s2[seg][z, 0:3] = a.astype(bf16)
        if seg == 2:
            for k in range(1, 16):
                d1[k].wait_recv()
                t = t1[k].astype(f32)
                tacc[...] += t[:8] + t[8:]
            s2[seg][z, 3] = split(tacc[...])
        cs = []
        for k in range(1, 8):
            c = send(s2[seg].at[z], s2[seg].at[z], p2s.at[seg, k], p2r.at[seg, k], depth(k))
            c.start()
            cs.append(c)
        c2.append(cs)

    mine = core * 16 + me

    def finish(seg):
        for k in range(1, 8):
            fr = lax.rem(z + 8 - k, 8)
            send(s2[seg].at[fr], s2[seg].at[fr], p2s.at[seg, k], p2r.at[seg, k], depth(k)).wait_recv()
        a = s2[seg][0].astype(f32)
        for t in range(1, 8):
            a = a + s2[seg][t].astype(f32)
        out[seg][mine, 0:3] = a[0:3].astype(bf16)
        if seg == 2:
            out[seg][mine, 3] = split(a[3, :8] + a[3, 8:])
        for k in range(1, 16):
            c = send(out[seg].at[mine], out[seg].at[mine], p4s.at[seg, k], p4r.at[seg, k], plane(k))
            c.start()
            c4.append(c)

    def hand_over(seg):
        for k in range(1, 16):
            f = core * 16 + plane_from(k)
            send(out[seg].at[f], out[seg].at[f], p4s.at[seg, k], p4r.at[seg, k], plane(k)).wait_recv()
        half = pl.ds(core * 16, 16)
        c = send(out[seg].at[half], out[seg].at[half], p5s.at[seg], p5r.at[seg], sib)
        c.start()
        c5.append(c)

    gn = dot(gq[...], wqkv[...], 1, 1).astype(bf16).astype(f32)
    xh = xhat[...]
    a = jnp.sum(gn * xh, axis=0, keepdims=True)
    b = jnp.sum(gn, axis=0, keepdims=True)
    for n in range(3):
        small[n : n + 1] = a[:, 128 * n : 128 * n + 128]
        small[3 + n : 4 + n] = b[:, 128 * n : 128 * n + 128]

    for seg in range(3):
        spread(seg)

    gg = gn * gain[...].reshape(1, 384)
    m1 = jnp.sum(gg, axis=1, keepdims=True) * (1.0 / 384)
    m2 = jnp.sum(gg * xh, axis=1, keepdims=True) * (1.0 / 384)
    gsh[...] = ((gg - m1 - xh * m2) * rstd[...]).astype(bf16)
    hbox[...] = dot(q2[...], gsh[...]).astype(bf16)
    back = []
    for i, (d, (lo, n)) in enumerate(zip(((rp, z, scene), (row, zp, scene), (rp, zp, scene)), pieces)):
        c = send(hbox.at[pl.ds(lo, n)], hout.at[pl.ds(lo, n)], bs.at[i], br.at[i], d)
        c.start()
        back.append(c)
    gl[...] = dot(q1[...], gsh[...]).astype(bf16)

    ones = jnp.ones((16, 512), bf16)
    sq = dot(ones, gq[...])[0:1]
    sp = dot(ones, up[...])[0:1]
    for n in range(9):
        small[6 + n : 7 + n] = sq[:, 128 * n : 128 * n + 128]
    for n in range(3):
        small[15 + n : 16 + n] = sp[:, 128 * n : 128 * n + 128]
    d = jnp.concatenate([gtab[p // 2, :, (p % 2) * 128 : (p % 2) * 128 + 128] for p in range(6)], axis=0)
    hi = d.astype(bf16)
    lo = (d - hi.astype(f32)).astype(bf16)
    eab = jnp.concatenate([ea[0], ea[1]], axis=0).astype(bf16)
    erb = er[...].astype(bf16)
    hi, lo = dot(hi, eab, 1, 1).astype(bf16), dot(lo, eab, 1, 1).astype(bf16)
    for pair in range(6):
        rows = slice(56 * pair, 56 * pair + 56)
        r = dot(erb, hi[rows]) + dot(erb, lo[rows])
        for half in range(2):
            h = 2 * pair + half
            wide = jnp.concatenate([r[:, 128 * half : 128 * half + 128], jnp.zeros((96, 128), f32)], axis=1)
            wide = pltpu.roll(wide, 248, 1, stride=1, stride_axis=0)
            u_h = jnp.sum(wide, axis=0, keepdims=True)
            small[18 + 2 * h : 19 + 2 * h] = u_h[:, :128]
            small[19 + 2 * h : 20 + 2 * h] = u_h[:, 128:]
    small[42:48] = jnp.zeros((6, 128), f32)
    for c in range(32):
        sg[c] = split(small[8 * c : 8 * c + 8]) if c < 6 else jnp.zeros((16, 128), bf16)
    d0 = send(sg.at[pl.ds((1 - core) * 16, 16)], t0, q0s, q0r, sib)
    d0.start()
    deepen(0)
    d0.wait_recv()
    for k in order:
        c = chunk(k)
        total = sg[core * 16 + c].astype(f32) + t0[c].astype(f32)
        total = total[:8] + total[8:]
        if k:
            ts[c] = split(total)
            d1[k] = send(ts.at[c], t1.at[k], q1s.at[k], q1r.at[k], plane(k))
            d1[k].start()
        else:
            tacc[...] = total
    deepen(1)
    finish(0)
    deepen(2)
    finish(1)
    hand_over(0)
    finish(2)
    hand_over(1)
    hand_over(2)
    for seg in range(3):
        other = pl.ds((1 - core) * 16, 16)
        send(out[seg].at[other], out[seg].at[other], p5s.at[seg], p5r.at[seg], sib).wait_recv()
    for c in back:
        c.wait_recv()
    for c in halo + back + c0 + c1[0] + c1[1] + c1[2] + [d0] + d1 + c2[0] + c2[1] + c2[2] + c4 + c5:
        if c is not None:
            c.wait_send()


def run_main(x, u, gain, shift, wqkv, bqkv, wproj, table, maps):
    pw1, pw2, ps, ea, eb, er, hm = maps
    c = lambda a: jnp.asarray(a, bf16)
    S, s, D = pltpu.VMEM, jax.ShapeDtypeStruct, pltpu.SemaphoreType.DMA
    sems = [D((n,)) for n in (6, 6, 3, 3, 3, 3)] + [D((3, 16)), D((3, 16)), D(()), D(()), D((16,)), D((16,))]
    sems += [D((3, 8)), D((3, 8)), D((3, 16)), D((3, 16)), D((3,)), D((3,))]
    j = jnp.asarray
    args = (x, u, c(ps), c(pw1), table, j(eb), j(ea), gain, shift, wqkv, bqkv, wproj, c(pw2), c(hm), c(pw2.T), c(pw1.T), j(er))
    return pl.pallas_call(
        main_kernel,
        out_shape=tuple(s((32, n, 16, 128), bf16) for n in (3, 3, 4)) + (s((392, 384), bf16), s((192, 384), bf16)),
        in_specs=[pl.BlockSpec(memory_space=pltpu.HBM)] * 17,
        out_specs=(V,) * 5,
        scratch_shapes=[S(a.shape, a.dtype) for a in args] + [D((17,))] + [
            S((392, 768), bf16), S((2, 192, 384), bf16), S((2, 192, 384), bf16),
            S((512, 384), f32), S((512, 1), f32), S((512, 384), bf16), S((512, 384), bf16),
            S((512, 1152), bf16), S((512, 384), bf16), S((512, 384), bf16), S((512, 1152), bf16),
            S((4, 3, 56, 256), f32), S((3, 56, 256), f32), S((16, 256), f32), S((48, 128), f32), S((512, 384), bf16),
            S((3, 32, 3, 16, 128), bf16), S((3, 16, 3, 16, 128), bf16), S((3, 16, 3, 16, 128), bf16),
        ] + [S((16, 3, 16, 128), bf16)] * 3 + [
            S((3, 3, 16, 128), f32), S((32, 16, 128), bf16), S((16, 16, 128), bf16), S((16, 16, 128), bf16),
            S((16, 16, 128), bf16), S((8, 128), f32),
        ] + [S((8, n, 16, 128), bf16) for n in (3, 3, 4)] + [S((192, 384), bf16)] + sems,
        compiler_params=pltpu.CompilerParams(collective_id=0, has_side_effects=True, vmem_limit_bytes=62 << 20),
    )(*args)


def final_kernel(
    scale, g0_in, g1_in, g2_in, u_in, gl_in, hr_in, q3_in,
    gx_out, a_out, b_out, wq_out, bq_out, wp_out, bp_out, t_out,
    g0, g1, g2, u, gl, hr, q3, load, small, tab,
):
    pairs = ((g0_in, g0), (g1_in, g1), (g2_in, g2), (u_in, u), (gl_in, gl), (hr_in, hr), (q3_in, q3))
    loads = [pltpu.make_async_copy(a, b, load.at[i]) for i, (a, b) in enumerate(pairs)]
    for c in loads:
        c.start()
    for c in loads:
        c.wait()
    got = gl[...].astype(f32) + dot(q3[...], hr[...])
    for p in range(196):
        gx_out[p] = (u[p].astype(f32) + got[2 * p : 2 * p + 2]).astype(bf16)
    for lb in range(12):
        dst, l = (wp_out, lb) if lb < 3 else (wq_out, lb - 3)
        g = (g0, g1, g2)[lb // 4]
        for i in range(24):
            t = (lb % 4) * 24 + i
            dst[16 * i : 16 * i + 16, 128 * l : 128 * l + 128] = g[t // 3, t % 3].astype(f32) * scale
    for c in range(6):
        t = g2[c, 3].astype(f32)
        small[8 * c : 8 * c + 8] = (t[:8] + t[8:]) * scale
    for n in range(3):
        d = pl.ds(128 * n, 128)
        a_out[d] = small[n]
        b_out[d] = small[3 + n]
        bp_out[d] = small[15 + n]
    for n in range(9):
        bq_out[pl.ds(128 * n, 128)] = small[6 + n]
    tab[...] = jnp.zeros_like(tab)
    for h in range(12):
        tab[h : h + 1, 0:128] = small[18 + 2 * h : 19 + 2 * h]
        tab[h : h + 1, 128:256] = small[19 + 2 * h : 20 + 2 * h]
    t_out[...] = tab[0:12, 0:169]


def run_final(scale, g0, g1, g2, u, gl, hr, maps):
    s = jax.ShapeDtypeStruct
    args = (g0, g1, g2, u, gl, hr, jnp.asarray(maps[2].T, bf16))
    return pl.pallas_call(
        functools.partial(final_kernel, scale),
        out_shape=(
            s((196, 2, 384), bf16), s((384,), f32), s((384,), f32), s((384, 1152), f32),
            s((1152,), f32), s((384, 384), f32), s((384,), f32), s((12, 169), f32),
        ),
        in_specs=[pl.BlockSpec(memory_space=pltpu.HBM)] * 7,
        out_specs=(V,) * 8,
        scratch_shapes=[pltpu.VMEM(a.shape, a.dtype) for a in args]
        + [pltpu.SemaphoreType.DMA((7,)), pltpu.VMEM((48, 128), f32), pltpu.VMEM((16, 256), f32)],
        compiler_params=pltpu.CompilerParams(vmem_limit_bytes=62 << 20),
    )(*args)


def on_device(features, grad_out, norm_gain, norm_shift, qkv_weight, qkv_bias, proj_weight, bias_table):
    maps = index_maps()
    x = features.transpose(1, 2, 0, 3).reshape(196, 2, 384)
    u = grad_out.transpose(1, 2, 0, 3).reshape(196, 2, 384)
    g0, g1, g2, gl, hr = run_main(x, u, norm_gain, norm_shift, qkv_weight, qkv_bias, proj_weight, bias_table.T, maps)
    scale = 1.0 / math.sqrt(8 * 112 * 112)
    gx, a, b, wq, bq, wp, bp, t = run_final(scale, g0, g1, g2, u, gl, hr, maps)
    return gx.reshape(14, 14, 2, 384).transpose(2, 0, 1, 3), a, b, wq, bq, wp, bp, t.T


def solution(mesh):
    return jax.shard_map(
        on_device,
        mesh=mesh,
        in_specs=(P("scene", "row", "col", None),) * 2 + (P(),) * 6,
        out_specs=(P("scene", "row", "col", None),) + (P(),) * 7,
        check_vma=False,
    )
```

```python
import functools
import math

import jax
import jax.numpy as jnp
import numpy as np
from jax import lax
from jax.experimental import pallas as pl
from jax.experimental.pallas import tpu as pltpu
from jax.sharding import PartitionSpec as P

WIN, SHIFT, NORM_EPS, MASKED = 7, 3, 1e-05, -1e30
LOG2E = 1.4426950408889634
UNROLL = 4
HIGH = lax.Precision.HIGHEST
MESH = pl.DeviceIdType.MESH
f32, bf16 = jnp.float32, jnp.bfloat16
V = pl.BlockSpec(memory_space=pltpu.VMEM)


def index_maps():
    pw1 = np.zeros((512, 392), np.float32)
    pw2 = np.zeros((512, 192), np.float32)
    ps = np.zeros((192, 392), np.float32)
    for s in range(2):
        for i in range(14):
            for j in range(14):
                w = (s * 2 + i // 7) * 2 + j // 7
                t = 64 * w + (i % 7) * 7 + j % 7
                flat = lambda a, b: (a * 14 + b) * 2 + s
                if i < 11 and j < 11:
                    pw1[t, flat(i + 3, j + 3)] = 1
                    continue
                if i >= 11 and j < 11:
                    slot, src = s * 33 + (i - 11) * 11 + j, flat(i - 11, j + 3)
                elif i < 11:
                    slot, src = 80 + s * 33 + i * 3 + j - 11, flat(i + 3, j - 11)
                else:
                    slot, src = 160 + s * 9 + (i - 11) * 3 + j - 11, flat(i - 11, j - 11)
                pw2[t, slot] = 1
                ps[slot, src] = 1
    ea = np.zeros((2, 128, 128), np.float32)
    eb = np.zeros((56, 96), np.float32)
    er = np.zeros((96, 56), np.float32)
    for a in range(49):
        off = (a // 7) * 13 + a % 7
        ea[0, off, a] = 1
        ea[1, off, 64 + a] = 1
        eb[a, off] = 1
        er[92 - off, a] = 1
    hm = (np.arange(256)[:, None] // 64 == np.arange(128)[None, :] // 32).astype(np.float32)
    return pw1, pw2, ps, ea, eb, er, hm


def place():
    row, z, scene = lax.axis_index("row"), lax.axis_index("col"), lax.axis_index("scene")
    x = (row // 4) * 2 + scene // 2
    return x, row % 4, z, scene % 2


def at(x, y, z, core):
    return ((x // 2) * 4 + y, z, (x % 2) * 2 + core)


def dot(a, b, ca=1, cb=0, **kw):
    return lax.dot_general(a, b, (((ca,), (cb,)), ((), ())), preferred_element_type=f32, **kw)


def split(t):
    hi = t.astype(bf16).astype(f32)
    return jnp.concatenate([hi, t - hi], axis=0).astype(bf16)


def main_kernel(
    x_in, u_in, ps_in, pw1_in, table_in, eb_in, ea_in, gain_in, shift_in, wqkv_in, bqkv_in, wproj_in, pw2_in, hm_in,
    q2_in, q1_in, er_in,
    out0_o, out1_o, out2_o, gl_o, hout_o,
    out0, out1, out2, gl, hout, store,
    x, u, ps, pw1, table, eb, ea, gain, shift, wqkv, bqkv, wproj, pw2, hm, q2, q1, er, load,
    flat, box, rx, xhat, rstd, norm, up, qkv, gat, attn, gq, tvar, gtab, tab, small, gsh,
    g, r0, s1, r1_0, r1_1, r1_2, acc, sg, t0, ts, t1, tacc, s2_0, s2_1, s2_2, hbox,
    hs, hr, bs, br, p0s, p0r, p1s, p1r, q0s, q0r, q1s, q1r, p2s, p2r, p4s, p4r, p5s, p5r, p6s, p6r,
):
    px, py, z, core = place()
    me = px * 4 + py
    row, scene = lax.axis_index("row"), lax.axis_index("scene")
    rm, zm = lax.rem(row + 7, 8), lax.rem(z + 7, 8)
    rp, zp = lax.rem(row + 1, 8), lax.rem(z + 1, 8)
    sib = at(px, py, z, 1 - core)

    def plane(k):
        return at(lax.rem(px + k // 4, 4), lax.rem(py + k % 4, 4), z, core)

    def plane_from(k):
        return lax.rem(px + 4 - k // 4, 4) * 4 + lax.rem(py + 4 - k % 4, 4)

    def depth(k):
        return at(px, py, lax.rem(z + k, 8), core)

    def send(src, dst, ss, rs, dev):
        return pltpu.make_async_remote_copy(
            src_ref=src, dst_ref=dst, send_sem=ss, recv_sem=rs, device_id=dev, device_id_type=MESH
        )

    bar = pltpu.get_barrier_semaphore()
    peers = [sib] + [plane(k) for k in range(1, 16)] + [depth(k) for k in range(1, 8)]
    peers += [(rm, zm, scene), (rp, zp, scene)]
    for d in peers:
        pl.semaphore_signal(bar, inc=1, device_id=d, device_id_type=MESH)

    loads = [
        pltpu.make_async_copy(a, b, load.at[i])
        for i, (a, b) in enumerate(
            (
                (x_in, x), (u_in, u), (ps_in, ps), (pw1_in, pw1), (table_in, table), (eb_in, eb), (ea_in, ea),
                (gain_in, gain), (shift_in, shift), (wqkv_in, wqkv), (bqkv_in, bqkv), (wproj_in, wproj),
                (pw2_in, pw2), (hm_in, hm), (q2_in, q2), (q1_in, q1), (er_in, er),
            )
        )
    ]
    for c in loads:
        c.start()
    for c in loads[:3]:
        c.wait()
    for p in range(196):
        flat[2 * p : 2 * p + 2, 0:384] = x[p]
        flat[2 * p : 2 * p + 2, 384:768] = u[p]
    box[0] = dot(ps[...], flat[:, 0:384]).astype(bf16)
    box[1] = dot(ps[...], flat[:, 384:768]).astype(bf16)
    pl.semaphore_wait(bar, len(peers))
    pieces = ((0, 80), (80, 80), (160, 32))
    halo = []
    for h in range(2):
        for i, (d, (lo, n)) in enumerate(zip(((rm, z, scene), (row, zm, scene), (rm, zm, scene)), pieces)):
            i = 3 * h + i
            c = send(box.at[h, pl.ds(lo, n)], rx.at[h, pl.ds(lo, n)], hs.at[i], hr.at[i], d)
            c.start()
            halo.append(c)
    for c in loads[3:]:
        c.wait()

    tab[...] = jnp.zeros_like(tab)
    tab[0:12, 0:169] = table[...] * LOG2E
    heads = pltpu.roll(tab[...], 4, 1)
    for pair in range(6):
        parts = []
        for half in range(2):
            h = 2 * pair + half
            wide = jnp.broadcast_to(heads[h : h + 1], (96, 256))
            wide = pltpu.roll(wide, 168, 1, stride=1, stride_axis=0)[:, :128]
            rows = dot(eb[...], wide, precision=HIGH)
            parts.append(dot(rows, ea[half], precision=HIGH))
        lo = (pair % 2) * 128
        tvar[0, pair // 2, :, lo : lo + 128] = parts[0] + parts[1]
    key = lax.broadcasted_iota(jnp.int32, (56, 256), 0)
    query = lax.broadcasted_iota(jnp.int32, (56, 256), 1) & 63

    def low(t):
        return (t >= 28).astype(jnp.int32), ((t - 7 * ((t * 37) >> 8)) >= 4).astype(jnp.int32)

    (ky, kx), (qy, qx_) = low(key), low(query)
    pad = key >= 49
    bad_row = ((ky != qy) & (query < 49)) & (row == 7)
    bad_col = ((kx != qx_) & (query < 49)) & (z == 7)
    for grp in range(3):
        t = jnp.where(pad, MASKED, tvar[0, grp])
        tvar[0, grp] = t
        tr = jnp.where(bad_row, MASKED, t)
        tvar[1, grp] = jnp.where(bad_col, MASKED, t)
        tvar[2, grp] = tr
        tvar[3, grp] = jnp.where(bad_col, MASKED, tr)
    gtab[...] = jnp.zeros_like(gtab)
    gq[...] = jnp.zeros_like(gq)

    v = dot(pw1[...], flat[:, 0:384])
    for c in halo[:3]:
        c.wait_recv()
    v = v + dot(pw2[...], rx[0])
    cen = v - jnp.sum(v, axis=1, keepdims=True) * (1.0 / 384)
    inv = lax.rsqrt(jnp.sum(cen * cen, axis=1, keepdims=True) * (1.0 / 384) + NORM_EPS)
    rstd[...] = inv
    xh = cen * inv
    xhat[...] = xh
    norm[...] = (xh * gain[...].reshape(1, 384) + shift[...].reshape(1, 384)).astype(bf16)
    for n in range(3):
        lanes = slice(384 * n, 384 * n + 384)
        qkv[:, lanes] = (dot(norm[...], wqkv[:, lanes]) + bqkv[...].reshape(1, 1152)[:, lanes]).astype(bf16)
    v = dot(pw1[...], flat[:, 384:768])
    for c in halo[3:]:
        c.wait_recv()
    up[...] = (v + dot(pw2[...], rx[1])).astype(bf16)
    gat[...] = dot(up[...], wproj[...], 1, 1).astype(bf16)

    scale = 32**-0.5
    lane = lax.broadcasted_iota(jnp.int32, (64, 128), 1)

    def merge(r):
        return jnp.where(
            lane < 32, r[0:64], jnp.where(lane < 64, r[64:128], jnp.where(lane < 96, r[128:192], r[192:256]))
        )

    def window(w, carry):
        base = pl.multiple_of(w * 64, 64)
        var = lax.rem(w, 4)
        for grp in range(3):
            lanes = [slice(384 * n + 128 * grp, 384 * n + 128 * grp + 128) for n in range(3)]
            q = qkv[pl.ds(base, 64), lanes[0]]
            k = qkv[pl.ds(base, 56), lanes[1]]
            vv = qkv[pl.ds(base, 56), lanes[2]]
            ga = gat[pl.ds(base, 64), lanes[0]]
            qx = jnp.concatenate([q, q, q, q], axis=0) * hm[...]
            gx = jnp.concatenate([ga, ga, ga, ga], axis=0) * hm[...]
            s = dot(k, qx, 1, 1) * (scale * LOG2E) + tvar[var, grp]
            e = jnp.exp2(s - jnp.max(s, axis=0, keepdims=True))
            p = e * (1.0 / jnp.sum(e, axis=0, keepdims=True))
            pb = p.astype(bf16)
            attn[pl.ds(base, 64), lanes[0]] = merge(dot(pb, vv, 0, 0)).astype(bf16)
            dp = dot(vv, gx, 1, 1)
            ds = p * (dp - jnp.sum(dp * p, axis=0, keepdims=True))
            gtab[grp] += ds
            db = ds.astype(bf16)
            gq[pl.ds(base, 64), lanes[0]] = (merge(dot(db, k, 0, 0)) * scale).astype(bf16)
            gq[pl.ds(base, 56), lanes[1]] = (dot(db, qx) * scale).astype(bf16)
            gq[pl.ds(base, 56), lanes[2]] = dot(pb, gx).astype(bf16)
        return carry

    def windows(i, carry):
        for j in range(UNROLL):
            window(i * UNROLL + j, carry)
        return carry

    lax.fori_loop(0, 8 // UNROLL, windows, 0)

    out, r1, s2 = (out0, out1, out2), (r1_0, r1_1, r1_2), (s2_0, s2_1, s2_2)
    hops = lambda k: min(k // 4, 4 - k // 4) + min(k % 4, 4 - k % 4)
    order = sorted(range(16), key=hops, reverse=True)
    far = (4, 3, 5, 2, 6, 1, 7)
    c0, c1, c2, c4, c5, d1 = [], [], [], [], [], [None] * 16

    def chunk(k):
        return lax.rem(px + k // 4, 4) * 4 + lax.rem(py + k % 4, 4)

    for seg in range(3):
        for n in range(4):
            lb = 4 * seg + n
            if lb < 3:
                m = dot(attn[...], up[:, 128 * lb : 128 * lb + 128], 0, 0)
            else:
                m = dot(norm[...], gq[:, 128 * (lb - 3) : 128 * (lb - 3) + 128], 0, 0)
            for i in range(24):
                t = n * 24 + i
                g[seg, t // 3, t % 3] = m[16 * i : 16 * i + 16].astype(bf16)
        c = send(g.at[seg, pl.ds((1 - core) * 16, 16)], r0.at[seg], p0s.at[seg], p0r.at[seg], sib)
        c.start()
        c0.append(c)

    def spread(seg):
        c0[seg].wait_recv()
        cs = [None] * 16
        for k in order:
            c = chunk(k)
            total = g[seg, core * 16 + c].astype(f32) + r0[seg, c].astype(f32)
            if k:
                s1[seg, c] = total.astype(bf16)
                cs[k] = send(s1.at[seg, c], r1[seg].at[k], p1s.at[seg, k], p1r.at[seg, k], plane(k))
                cs[k].start()
            else:
                acc[seg] = total
        c1.append(cs)

    def deepen(seg):
        a = acc[seg]
        for k in range(1, 16):
            c1[seg][k].wait_recv()
            a = a + r1[seg][k].astype(f32)
        s2[seg][z, 0:3] = a.astype(bf16)
        if seg == 2:
            for k in range(1, 16):
                d1[k].wait_recv()
                t = t1[k].astype(f32)
                tacc[...] += t[:8] + t[8:]
            s2[seg][z, 3] = split(tacc[...])
        cs = []
        for k in far:
            c = send(s2[seg].at[z], s2[seg].at[z], p2s.at[seg, k], p2r.at[seg, k], depth(k))
            c.start()
            cs.append(c)
        c2.append(cs)

    mine = core * 16 + me

    def finish(seg):
        for k in range(1, 8):
            fr = lax.rem(z + 8 - k, 8)
            send(s2[seg].at[fr], s2[seg].at[fr], p2s.at[seg, k], p2r.at[seg, k], depth(k)).wait_recv()
        a = s2[seg][0].astype(f32)
        for t in range(1, 8):
            a = a + s2[seg][t].astype(f32)
        out[seg][mine, 0:3] = a[0:3].astype(bf16)
        if seg == 2:
            out[seg][mine, 3] = split(a[3, :8] + a[3, 8:])
        for k in order[:15]:
            c = send(out[seg].at[mine], out[seg].at[mine], p4s.at[seg, k], p4r.at[seg, k], plane(k))
            c.start()
            c4.append(c)

    def hand_over(seg):
        if seg < 2:
            for k in range(1, 16):
                f = core * 16 + plane_from(k)
                send(out[seg].at[f], out[seg].at[f], p4s.at[seg, k], p4r.at[seg, k], plane(k)).wait_recv()
            half = pl.ds(core * 16, 16)
            c = send(out[seg].at[half], out[seg].at[half], p5s.at[seg], p5r.at[seg], sib)
            c.start()
            c5.append(c)
            return
        for k in [0] + order[14::-1]:
            f = core * 16 + plane_from(k)
            if k:
                send(out[seg].at[f], out[seg].at[f], p4s.at[seg, k], p4r.at[seg, k], plane(k)).wait_recv()
            c = send(out[seg].at[f], out[seg].at[f], p6s.at[k], p6r.at[k], sib)
            c.start()
            c5.append(c)

    def keep(i, src, dst):
        c = pltpu.make_async_copy(src, dst, store.at[i])
        c.start()
        kept.append(c)

    kept = []
    spread(0)

    gn = dot(gq[...], wqkv[...], 1, 1).astype(bf16).astype(f32)
    xh = xhat[...]
    spread(1)
    spread(2)
    a = jnp.sum(gn * xh, axis=0, keepdims=True)
    b = jnp.sum(gn, axis=0, keepdims=True)
    for n in range(3):
        small[n : n + 1] = a[:, 128 * n : 128 * n + 128]
        small[3 + n : 4 + n] = b[:, 128 * n : 128 * n + 128]

    ones = jnp.ones((16, 512), bf16)
    sq = dot(ones, gq[...])[0:1]
    sp = dot(ones, up[...])[0:1]
    for n in range(9):
        small[6 + n : 7 + n] = sq[:, 128 * n : 128 * n + 128]
    for n in range(3):
        small[15 + n : 16 + n] = sp[:, 128 * n : 128 * n + 128]
    d = jnp.concatenate([gtab[p // 2, :, (p % 2) * 128 : (p % 2) * 128 + 128] for p in range(6)], axis=0)
    hi = d.astype(bf16)
    lo = (d - hi.astype(f32)).astype(bf16)
    eab = jnp.concatenate([ea[0], ea[1]], axis=0).astype(bf16)
    erb = er[...].astype(bf16)
    hi, lo = dot(hi, eab, 1, 1).astype(bf16), dot(lo, eab, 1, 1).astype(bf16)
    for pair in range(6):
        rows = slice(56 * pair, 56 * pair + 56)
        r = dot(erb, hi[rows]) + dot(erb, lo[rows])
        for half in range(2):
            h = 2 * pair + half
            wide = jnp.concatenate([r[:, 128 * half : 128 * half + 128], jnp.zeros((96, 128), f32)], axis=1)
            wide = pltpu.roll(wide, 248, 1, stride=1, stride_axis=0)
            u_h = jnp.sum(wide, axis=0, keepdims=True)
            small[18 + 2 * h : 19 + 2 * h] = u_h[:, :128]
            small[19 + 2 * h : 20 + 2 * h] = u_h[:, 128:]
    small[42:48] = jnp.zeros((6, 128), f32)
    for c in range(32):
        sg[c] = split(small[8 * c : 8 * c + 8]) if c < 6 else jnp.zeros((16, 128), bf16)
    d0 = send(sg.at[pl.ds((1 - core) * 16, 16)], t0, q0s, q0r, sib)
    d0.start()
    deepen(0)
    d0.wait_recv()
    for k in order:
        c = chunk(k)
        total = sg[core * 16 + c].astype(f32) + t0[c].astype(f32)
        total = total[:8] + total[8:]
        if k:
            ts[c] = split(total)
            d1[k] = send(ts.at[c], t1.at[k], q1s.at[k], q1r.at[k], plane(k))
            d1[k].start()
        else:
            tacc[...] = total
    deepen(1)
    gg = gn * gain[...].reshape(1, 384)
    m1 = jnp.sum(gg, axis=1, keepdims=True) * (1.0 / 384)
    m2 = jnp.sum(gg * xh, axis=1, keepdims=True) * (1.0 / 384)
    gsh[...] = ((gg - m1 - xh * m2) * rstd[...]).astype(bf16)
    hbox[...] = dot(q2[...], gsh[...]).astype(bf16)
    back = []
    for i, (d, (lo, n)) in enumerate(zip(((rp, z, scene), (row, zp, scene), (rp, zp, scene)), pieces)):
        c = send(hbox.at[pl.ds(lo, n)], hout.at[pl.ds(lo, n)], bs.at[i], br.at[i], d)
        c.start()
        back.append(c)
    gl[...] = dot(q1[...], gsh[...]).astype(bf16)

    keep(3, gl, gl_o)
    finish(0)
    deepen(2)
    finish(1)
    hand_over(0)
    finish(2)
    hand_over(1)
    for c in back:
        c.wait_recv()
    keep(4, hout, hout_o)
    half, other = pl.ds(core * 16, 16), pl.ds((1 - core) * 16, 16)
    send(out0.at[half], out0.at[other], p5s.at[0], p5r.at[0], sib).wait_recv()
    keep(0, out0, out0_o)
    hand_over(2)
    send(out1.at[half], out1.at[other], p5s.at[1], p5r.at[1], sib).wait_recv()
    keep(1, out1, out1_o)
    for k in [0] + order[14::-1]:
        f = (1 - core) * 16 + plane_from(k)
        send(out2.at[f], out2.at[f], p6s.at[k], p6r.at[k], sib).wait_recv()
    keep(2, out2, out2_o)
    for c in halo + back + c0 + c1[0] + c1[1] + c1[2] + [d0] + d1 + c2[0] + c2[1] + c2[2] + c4 + c5:
        if c is not None:
            c.wait_send()
    for c in kept:
        c.wait()


def run_main(x, u, gain, shift, wqkv, bqkv, wproj, table, maps):
    pw1, pw2, ps, ea, eb, er, hm = maps
    c = lambda a: jnp.asarray(a, bf16)
    S, s, D = pltpu.VMEM, jax.ShapeDtypeStruct, pltpu.SemaphoreType.DMA
    sems = [D((n,)) for n in (6, 6, 3, 3, 3, 3)] + [D((3, 16)), D((3, 16)), D(()), D(()), D((16,)), D((16,))]
    sems += [D((3, 8)), D((3, 8)), D((3, 16)), D((3, 16)), D((2,)), D((2,)), D((16,)), D((16,))]
    j = jnp.asarray
    args = (x, u, c(ps), c(pw1), table, j(eb), j(ea), gain, shift, wqkv, bqkv, wproj, c(pw2), c(hm), c(pw2.T), c(pw1.T), j(er))
    outs = tuple(s((32, n, 16, 128), bf16) for n in (3, 3, 4)) + (s((392, 384), bf16), s((192, 384), bf16))
    return pl.pallas_call(
        main_kernel,
        out_shape=outs,
        in_specs=[pl.BlockSpec(memory_space=pltpu.HBM)] * 17,
        out_specs=(pl.BlockSpec(memory_space=pltpu.HBM),) * 5,
        scratch_shapes=[S(o.shape, o.dtype) for o in outs] + [D((5,))] + [S(a.shape, a.dtype) for a in args] + [D((17,))] + [
            S((392, 768), bf16), S((2, 192, 384), bf16), S((2, 192, 384), bf16),
            S((512, 384), f32), S((512, 1), f32), S((512, 384), bf16), S((512, 384), bf16),
            S((512, 1152), bf16), S((512, 384), bf16), S((512, 384), bf16), S((512, 1152), bf16),
            S((4, 3, 56, 256), f32), S((3, 56, 256), f32), S((16, 256), f32), S((48, 128), f32), S((512, 384), bf16),
            S((3, 32, 3, 16, 128), bf16), S((3, 16, 3, 16, 128), bf16), S((3, 16, 3, 16, 128), bf16),
        ] + [S((16, 3, 16, 128), bf16)] * 3 + [
            S((3, 3, 16, 128), f32), S((32, 16, 128), bf16), S((16, 16, 128), bf16), S((16, 16, 128), bf16),
            S((16, 16, 128), bf16), S((8, 128), f32),
        ] + [S((8, n, 16, 128), bf16) for n in (3, 3, 4)] + [S((192, 384), bf16)] + sems,
        compiler_params=pltpu.CompilerParams(collective_id=0, has_side_effects=True, vmem_limit_bytes=62 << 20),
    )(*args)


def final_kernel(
    scale, g0_in, g1_in, g2_in, u_in, gl_in, hr_in, q3_in,
    gx_o, wq_o, wp_o, a_out, b_out, bq_out, bp_out, t_out,
    g0, g1, g2, u, gl, hr, q3, load, gx, wq, wp, store, small, tab,
):
    pairs = ((g0_in, g0), (g1_in, g1), (g2_in, g2), (hr_in, hr), (q3_in, q3), (gl_in, gl), (u_in, u))
    loads = [pltpu.make_async_copy(a, b, load.at[i]) for i, (a, b) in enumerate(pairs)]
    for c in loads:
        c.start()
    stores = []

    def put(src, dst):
        c = pltpu.make_async_copy(src, dst, store.at[len(stores)])
        c.start()
        stores.append(c)

    for seg, g in enumerate((g0, g1, g2)):
        loads[seg].wait()
        for n in range(4):
            lb = 4 * seg + n
            dst, l = (wp, lb) if lb < 3 else (wq, lb - 3)
            for i in range(24):
                t = n * 24 + i
                dst[16 * i : 16 * i + 16, 128 * l : 128 * l + 128] = g[t // 3, t % 3].astype(f32) * scale
        lanes = (pl.ds(0, 128), pl.ds(128, 512), pl.ds(640, 512))[seg]
        put(wq.at[:, lanes], wq_o.at[:, lanes])
        if seg == 0:
            put(wp, wp_o)
    for c in loads[3:]:
        c.wait()
    got = gl[...].astype(f32) + dot(q3[...], hr[...])
    for p in range(196):
        gx[p] = (u[p].astype(f32) + got[2 * p : 2 * p + 2]).astype(bf16)
    put(gx, gx_o)
    for c in range(6):
        t = g2[c, 3].astype(f32)
        small[8 * c : 8 * c + 8] = (t[:8] + t[8:]) * scale
    for n in range(3):
        d = pl.ds(128 * n, 128)
        a_out[d] = small[n]
        b_out[d] = small[3 + n]
        bp_out[d] = small[15 + n]
    for n in range(9):
        bq_out[pl.ds(128 * n, 128)] = small[6 + n]
    tab[...] = jnp.zeros_like(tab)
    for h in range(12):
        tab[h : h + 1, 0:128] = small[18 + 2 * h : 19 + 2 * h]
        tab[h : h + 1, 128:256] = small[19 + 2 * h : 20 + 2 * h]
    t_out[...] = tab[0:12, 0:169]
    for c in stores:
        c.wait()


def run_final(scale, g0, g1, g2, u, gl, hr, maps):
    s = jax.ShapeDtypeStruct
    args = (g0, g1, g2, u, gl, hr, jnp.asarray(maps[2].T, bf16))
    big = (s((196, 2, 384), bf16), s((384, 1152), f32), s((384, 384), f32))
    return pl.pallas_call(
        functools.partial(final_kernel, scale),
        out_shape=big
        + (s((384,), f32), s((384,), f32), s((1152,), f32), s((384,), f32), s((12, 169), f32)),
        in_specs=[pl.BlockSpec(memory_space=pltpu.HBM)] * 7,
        out_specs=(pl.BlockSpec(memory_space=pltpu.HBM),) * 3 + (V,) * 5,
        scratch_shapes=[pltpu.VMEM(a.shape, a.dtype) for a in args]
        + [pltpu.SemaphoreType.DMA((7,))]
        + [pltpu.VMEM(a.shape, a.dtype) for a in big]
        + [pltpu.SemaphoreType.DMA((5,)), pltpu.VMEM((48, 128), f32), pltpu.VMEM((16, 256), f32)],
        compiler_params=pltpu.CompilerParams(vmem_limit_bytes=62 << 20),
    )(*args)


def on_device(features, grad_out, norm_gain, norm_shift, qkv_weight, qkv_bias, proj_weight, bias_table):
    maps = index_maps()
    x = features.transpose(1, 2, 0, 3).reshape(196, 2, 384)
    u = grad_out.transpose(1, 2, 0, 3).reshape(196, 2, 384)
    g0, g1, g2, gl, hr = run_main(x, u, norm_gain, norm_shift, qkv_weight, qkv_bias, proj_weight, bias_table.T, maps)
    scale = 1.0 / math.sqrt(8 * 112 * 112)
    gx, wq, wp, a, b, bq, bp, t = run_final(scale, g0, g1, g2, u, gl, hr, maps)
    return gx.reshape(14, 14, 2, 384).transpose(2, 0, 1, 3), a, b, wq, bq, wp, bp, t.T


def solution(mesh):
    return jax.shard_map(
        on_device,
        mesh=mesh,
        in_specs=(P("scene", "row", "col", None),) * 2 + (P(),) * 6,
        out_specs=(P("scene", "row", "col", None),) + (P(),) * 7,
        check_vma=False,
    )
```

```python
import functools
import math

import jax
import jax.numpy as jnp
import numpy as np
from jax import lax
from jax.experimental import pallas as pl
from jax.experimental.pallas import tpu as pltpu
from jax.sharding import PartitionSpec as P

WIN, SHIFT, NORM_EPS, MASKED = 7, 3, 1e-05, -1e30
LOG2E = 1.4426950408889634
UNROLL = 8
HIGH = lax.Precision.HIGHEST
MESH = pl.DeviceIdType.MESH
f32, bf16 = jnp.float32, jnp.bfloat16
V = pl.BlockSpec(memory_space=pltpu.VMEM)


def index_maps():
    pw1 = np.zeros((512, 392), np.float32)
    pw2 = np.zeros((512, 192), np.float32)
    ps = np.zeros((192, 392), np.float32)
    for s in range(2):
        for i in range(14):
            for j in range(14):
                w = (s * 2 + i // 7) * 2 + j // 7
                t = 64 * w + (i % 7) * 7 + j % 7
                flat = lambda a, b: (a * 14 + b) * 2 + s
                if i < 11 and j < 11:
                    pw1[t, flat(i + 3, j + 3)] = 1
                    continue
                if i >= 11 and j < 11:
                    slot, src = s * 33 + (i - 11) * 11 + j, flat(i - 11, j + 3)
                elif i < 11:
                    slot, src = 80 + s * 33 + i * 3 + j - 11, flat(i + 3, j - 11)
                else:
                    slot, src = 160 + s * 9 + (i - 11) * 3 + j - 11, flat(i - 11, j - 11)
                pw2[t, slot] = 1
                ps[slot, src] = 1
    ea = np.zeros((2, 128, 128), np.float32)
    eb = np.zeros((56, 96), np.float32)
    er = np.zeros((96, 56), np.float32)
    for a in range(49):
        off = (a // 7) * 13 + a % 7
        ea[0, off, a] = 1
        ea[1, off, 64 + a] = 1
        eb[a, off] = 1
        er[92 - off, a] = 1
    hm = (np.arange(256)[:, None] // 64 == np.arange(128)[None, :] // 32).astype(np.float32)
    return pw1, pw2, ps, ea, eb, er, hm


def place():
    row, z, scene = lax.axis_index("row"), lax.axis_index("col"), lax.axis_index("scene")
    x = (row // 4) * 2 + scene // 2
    return x, row % 4, z, scene % 2


def at(x, y, z, core):
    return ((x // 2) * 4 + y, z, (x % 2) * 2 + core)


def dot(a, b, ca=1, cb=0, **kw):
    return lax.dot_general(a, b, (((ca,), (cb,)), ((), ())), preferred_element_type=f32, **kw)


def split(t):
    hi = t.astype(bf16).astype(f32)
    return jnp.concatenate([hi, t - hi], axis=0).astype(bf16)


def main_kernel(
    x_in, u_in, ps_in, pw1_in, table_in, eb_in, ea_in, gain_in, shift_in, wqkv_in, bqkv_in, wproj_in, pw2_in, hm_in,
    q2_in, q1_in, er_in,
    out0_o, out1_o, out2_o, gl_o, hout_o,
    out0, out1, out2, gl, hout, store,
    x, u, ps, pw1, table, eb, ea, gain, shift, wqkv, bqkv, wproj, pw2, hm, q2, q1, er, load,
    flat, box, rx, xhat, rstd, norm, up, qkv, gat, attn, gq, tvar, gtab, tab, small, gsh,
    g, r0, s1, r1_0, r1_1, r1_2, acc, sg, t0, ts, t1, tacc, s2_0, s2_1, s2_2, hbox,
    hs, hr, bs, br, p0s, p0r, p1s, p1r, q0s, q0r, q1s, q1r, p2s, p2r, p4s, p4r, p5s, p5r,
):
    px, py, z, core = place()
    me = px * 4 + py
    row, scene = lax.axis_index("row"), lax.axis_index("scene")
    rm, zm = lax.rem(row + 7, 8), lax.rem(z + 7, 8)
    rp, zp = lax.rem(row + 1, 8), lax.rem(z + 1, 8)
    sib = at(px, py, z, 1 - core)

    def plane(k):
        return at(lax.rem(px + k // 4, 4), lax.rem(py + k % 4, 4), z, core)

    def depth(k):
        return at(px, py, lax.rem(z + k, 8), core)

    def send(src, dst, ss, rs, dev):
        return pltpu.make_async_remote_copy(
            src_ref=src, dst_ref=dst, send_sem=ss, recv_sem=rs, device_id=dev, device_id_type=MESH
        )

    bar = pltpu.get_barrier_semaphore()
    peers = [sib] + [plane(k) for k in range(1, 16)] + [depth(k) for k in range(1, 8)]
    peers += [(rm, zm, scene), (rp, zp, scene)]
    for d in peers:
        pl.semaphore_signal(bar, inc=1, device_id=d, device_id_type=MESH)

    loads = [
        pltpu.make_async_copy(a, b, load.at[i])
        for i, (a, b) in enumerate(
            (
                (x_in, x), (u_in, u), (ps_in, ps), (pw1_in, pw1), (table_in, table), (eb_in, eb), (ea_in, ea),
                (gain_in, gain), (shift_in, shift), (wqkv_in, wqkv), (bqkv_in, bqkv), (wproj_in, wproj),
                (pw2_in, pw2), (hm_in, hm), (q2_in, q2), (q1_in, q1), (er_in, er),
            )
        )
    ]
    for c in loads:
        c.start()
    for c in loads[:3]:
        c.wait()
    for p in range(196):
        flat[2 * p : 2 * p + 2, 0:384] = x[p]
        flat[2 * p : 2 * p + 2, 384:768] = u[p]
    box[0] = dot(ps[...], flat[:, 0:384]).astype(bf16)
    box[1] = dot(ps[...], flat[:, 384:768]).astype(bf16)
    pl.semaphore_wait(bar, len(peers))
    pieces = ((0, 80), (80, 80), (160, 32))
    halo = []
    for h in range(2):
        for i, (d, (lo, n)) in enumerate(zip(((rm, z, scene), (row, zm, scene), (rm, zm, scene)), pieces)):
            i = 3 * h + i
            c = send(box.at[h, pl.ds(lo, n)], rx.at[h, pl.ds(lo, n)], hs.at[i], hr.at[i], d)
            c.start()
            halo.append(c)
    for c in loads[3:]:
        c.wait()

    tab[...] = jnp.zeros_like(tab)
    tab[0:12, 0:169] = table[...] * LOG2E
    heads = pltpu.roll(tab[...], 4, 1)
    for pair in range(6):
        parts = []
        for half in range(2):
            h = 2 * pair + half
            wide = jnp.broadcast_to(heads[h : h + 1], (96, 256))
            wide = pltpu.roll(wide, 168, 1, stride=1, stride_axis=0)[:, :128]
            rows = dot(eb[...], wide, precision=HIGH)
            parts.append(dot(rows, ea[half], precision=HIGH))
        lo = (pair % 2) * 128
        tvar[0, pair // 2, :, lo : lo + 128] = parts[0] + parts[1]
    key = lax.broadcasted_iota(jnp.int32, (56, 256), 0)
    query = lax.broadcasted_iota(jnp.int32, (56, 256), 1) & 63

    def low(t):
        return (t >= 28).astype(jnp.int32), ((t - 7 * ((t * 37) >> 8)) >= 4).astype(jnp.int32)

    (ky, kx), (qy, qx_) = low(key), low(query)
    pad = key >= 49
    bad_row = ((ky != qy) & (query < 49)) & (row == 7)
    bad_col = ((kx != qx_) & (query < 49)) & (z == 7)
    for grp in range(3):
        t = jnp.where(pad, MASKED, tvar[0, grp])
        tvar[0, grp] = t
        tr = jnp.where(bad_row, MASKED, t)
        tvar[1, grp] = jnp.where(bad_col, MASKED, t)
        tvar[2, grp] = tr
        tvar[3, grp] = jnp.where(bad_col, MASKED, tr)
    gtab[...] = jnp.zeros_like(gtab)
    gq[...] = jnp.zeros_like(gq)

    v = dot(pw1[...], flat[:, 0:384])
    for c in halo[:3]:
        c.wait_recv()
    v = v + dot(pw2[...], rx[0])
    cen = v - jnp.sum(v, axis=1, keepdims=True) * (1.0 / 384)
    inv = lax.rsqrt(jnp.sum(cen * cen, axis=1, keepdims=True) * (1.0 / 384) + NORM_EPS)
    rstd[...] = inv
    xh = cen * inv
    xhat[...] = xh
    norm[...] = (xh * gain[...].reshape(1, 384) + shift[...].reshape(1, 384)).astype(bf16)
    for n in range(3):
        lanes = slice(384 * n, 384 * n + 384)
        qkv[:, lanes] = (dot(norm[...], wqkv[:, lanes]) + bqkv[...].reshape(1, 1152)[:, lanes]).astype(bf16)
    v = dot(pw1[...], flat[:, 384:768])
    for c in halo[3:]:
        c.wait_recv()
    up[...] = (v + dot(pw2[...], rx[1])).astype(bf16)
    gat[...] = dot(up[...], wproj[...], 1, 1).astype(bf16)

    scale = 32**-0.5
    lane = lax.broadcasted_iota(jnp.int32, (64, 128), 1)

    def merge(r):
        return jnp.where(
            lane < 32, r[0:64], jnp.where(lane < 64, r[64:128], jnp.where(lane < 96, r[128:192], r[192:256]))
        )

    def window(w, carry):
        base = pl.multiple_of(w * 64, 64)
        var = lax.rem(w, 4)
        for grp in range(3):
            lanes = [slice(384 * n + 128 * grp, 384 * n + 128 * grp + 128) for n in range(3)]
            q = qkv[pl.ds(base, 64), lanes[0]]
            k = qkv[pl.ds(base, 56), lanes[1]]
            vv = qkv[pl.ds(base, 56), lanes[2]]
            ga = gat[pl.ds(base, 64), lanes[0]]
            qx = jnp.concatenate([q, q, q, q], axis=0) * hm[...]
            gx = jnp.concatenate([ga, ga, ga, ga], axis=0) * hm[...]
            s = dot(k, qx, 1, 1) * (scale * LOG2E) + tvar[var, grp]
            e = jnp.exp2(s - jnp.max(s, axis=0, keepdims=True))
            p = e * (1.0 / jnp.sum(e, axis=0, keepdims=True))
            pb = p.astype(bf16)
            attn[pl.ds(base, 64), lanes[0]] = merge(dot(pb, vv, 0, 0)).astype(bf16)
            dp = dot(vv, gx, 1, 1)
            ds = p * (dp - jnp.sum(dp * p, axis=0, keepdims=True))
            gtab[grp] += ds
            db = ds.astype(bf16)
            gq[pl.ds(base, 64), lanes[0]] = (merge(dot(db, k, 0, 0)) * scale).astype(bf16)
            gq[pl.ds(base, 56), lanes[1]] = (dot(db, qx) * scale).astype(bf16)
            gq[pl.ds(base, 56), lanes[2]] = dot(pb, gx).astype(bf16)
        return carry

    def windows(i, carry):
        for j in range(UNROLL):
            window(i * UNROLL + j, carry)
        return carry

    lax.fori_loop(0, 8 // UNROLL, windows, 0)

    out, r1, s2 = (out0, out1, out2), (r1_0, r1_1, r1_2), (s2_0, s2_1, s2_2)
    hops = lambda k: min(k // 4, 4 - k // 4) + min(k % 4, 4 - k % 4)
    order = sorted(range(16), key=hops, reverse=True)
    far = (4, 3, 5, 2, 6, 1, 7)
    c0, c5 = [], []

    def all_of(what, sem):
        pltpu.make_async_copy(what, what, sem).wait()

    def chunk(k):
        return lax.rem(px + k // 4, 4) * 4 + lax.rem(py + k % 4, 4)

    for seg in range(3):
        for n in range(4):
            lb = 4 * seg + n
            if lb < 3:
                m = dot(attn[...], up[:, 128 * lb : 128 * lb + 128], 0, 0)
            else:
                m = dot(norm[...], gq[:, 128 * (lb - 3) : 128 * (lb - 3) + 128], 0, 0)
            for i in range(24):
                t = n * 24 + i
                g[seg, t // 3, t % 3] = m[16 * i : 16 * i + 16].astype(bf16)
        c = send(g.at[seg, pl.ds((1 - core) * 16, 16)], r0.at[seg], p0s.at[seg], p0r.at[seg], sib)
        c.start()
        c0.append(c)

    def spread(seg):
        c0[seg].wait_recv()
        for k in order:
            c = chunk(k)
            total = g[seg, core * 16 + c].astype(f32) + r0[seg, c].astype(f32)
            if k:
                s1[seg, c] = total.astype(bf16)
                c = send(s1.at[seg, c], r1[seg].at[k], p1s.at[seg], p1r.at[seg], plane(k))
                c.start()
            else:
                acc[seg] = total

    def deepen(seg):
        a = acc[seg]
        all_of(r1[seg].at[pl.ds(1, 15)], p1r.at[seg])
        for k in range(1, 16):
            a = a + r1[seg][k].astype(f32)
        s2[seg][z, 0:3] = a.astype(bf16)
        if seg == 2:
            all_of(t1.at[pl.ds(1, 15)], q1r)
            for k in range(1, 16):
                t = t1[k].astype(f32)
                tacc[...] += t[:8] + t[8:]
            s2[seg][z, 3] = split(tacc[...])
        for k in far:
            c = send(s2[seg].at[z], s2[seg].at[z], p2s.at[seg], p2r.at[seg], depth(k))
            c.start()

    mine = core * 16 + me

    def finish(seg):
        all_of(s2[seg].at[pl.ds(0, 7)], p2r.at[seg])
        a = s2[seg][0].astype(f32)
        for t in range(1, 8):
            a = a + s2[seg][t].astype(f32)
        out[seg][mine, 0:3] = a[0:3].astype(bf16)
        if seg == 2:
            out[seg][mine, 3] = split(a[3, :8] + a[3, 8:])
        for k in order[:15]:
            c = send(out[seg].at[mine], out[seg].at[mine], p4s.at[seg], p4r.at[seg], plane(k))
            c.start()

    def hand_over(seg):
        all_of(out[seg].at[pl.ds(0, 15)], p4r.at[seg])
        half = pl.ds(core * 16, 16)
        c = send(out[seg].at[half], out[seg].at[half], p5s.at[seg], p5r.at[seg], sib)
        c.start()
        c5.append(c)

    def keep(i, src, dst):
        c = pltpu.make_async_copy(src, dst, store.at[i])
        c.start()
        kept.append(c)

    kept = []
    spread(0)

    gn = dot(gq[...], wqkv[...], 1, 1).astype(bf16).astype(f32)
    xh = xhat[...]
    spread(1)
    spread(2)
    a = jnp.sum(gn * xh, axis=0, keepdims=True)
    b = jnp.sum(gn, axis=0, keepdims=True)
    for n in range(3):
        small[n : n + 1] = a[:, 128 * n : 128 * n + 128]
        small[3 + n : 4 + n] = b[:, 128 * n : 128 * n + 128]

    ones = jnp.ones((16, 512), bf16)
    sq = dot(ones, gq[...])[0:1]
    sp = dot(ones, up[...])[0:1]
    for n in range(9):
        small[6 + n : 7 + n] = sq[:, 128 * n : 128 * n + 128]
    for n in range(3):
        small[15 + n : 16 + n] = sp[:, 128 * n : 128 * n + 128]
    d = jnp.concatenate([gtab[p // 2, :, (p % 2) * 128 : (p % 2) * 128 + 128] for p in range(6)], axis=0)
    hi = d.astype(bf16)
    lo = (d - hi.astype(f32)).astype(bf16)
    eab = jnp.concatenate([ea[0], ea[1]], axis=0).astype(bf16)
    erb = er[...].astype(bf16)
    hi, lo = dot(hi, eab, 1, 1).astype(bf16), dot(lo, eab, 1, 1).astype(bf16)
    for pair in range(6):
        rows = slice(56 * pair, 56 * pair + 56)
        r = dot(erb, hi[rows]) + dot(erb, lo[rows])
        for half in range(2):
            h = 2 * pair + half
            wide = jnp.concatenate([r[:, 128 * half : 128 * half + 128], jnp.zeros((96, 128), f32)], axis=1)
            wide = pltpu.roll(wide, 248, 1, stride=1, stride_axis=0)
            u_h = jnp.sum(wide, axis=0, keepdims=True)
            small[18 + 2 * h : 19 + 2 * h] = u_h[:, :128]
            small[19 + 2 * h : 20 + 2 * h] = u_h[:, 128:]
    small[42:48] = jnp.zeros((6, 128), f32)
    for c in range(32):
        sg[c] = split(small[8 * c : 8 * c + 8]) if c < 6 else jnp.zeros((16, 128), bf16)
    d0 = send(sg.at[pl.ds((1 - core) * 16, 16)], t0, q0s, q0r, sib)
    d0.start()
    deepen(0)
    d0.wait_recv()
    for k in order:
        c = chunk(k)
        total = sg[core * 16 + c].astype(f32) + t0[c].astype(f32)
        total = total[:8] + total[8:]
        if k:
            ts[c] = split(total)
            c = send(ts.at[c], t1.at[k], q1s, q1r, plane(k))
            c.start()
        else:
            tacc[...] = total
    deepen(1)
    gg = gn * gain[...].reshape(1, 384)
    m1 = jnp.sum(gg, axis=1, keepdims=True) * (1.0 / 384)
    m2 = jnp.sum(gg * xh, axis=1, keepdims=True) * (1.0 / 384)
    gsh[...] = ((gg - m1 - xh * m2) * rstd[...]).astype(bf16)
    hbox[...] = dot(q2[...], gsh[...]).astype(bf16)
    back = []
    for i, (d, (lo, n)) in enumerate(zip(((rp, z, scene), (row, zp, scene), (rp, zp, scene)), pieces)):
        c = send(hbox.at[pl.ds(lo, n)], hout.at[pl.ds(lo, n)], bs.at[i], br.at[i], d)
        c.start()
        back.append(c)
    gl[...] = dot(q1[...], gsh[...]).astype(bf16)

    keep(3, gl, gl_o)
    finish(0)
    deepen(2)
    finish(1)
    hand_over(0)
    finish(2)
    hand_over(1)
    for c in back:
        c.wait_recv()
    keep(4, hout, hout_o)
    half, other = pl.ds(core * 16, 16), pl.ds((1 - core) * 16, 16)
    send(out0.at[half], out0.at[other], p5s.at[0], p5r.at[0], sib).wait_recv()
    keep(0, out0, out0_o)
    hand_over(2)
    send(out1.at[half], out1.at[other], p5s.at[1], p5r.at[1], sib).wait_recv()
    keep(1, out1, out1_o)
    send(out2.at[half], out2.at[other], p5s.at[2], p5r.at[2], sib).wait_recv()
    keep(2, out2, out2_o)
    for c in halo + back + c0 + [d0] + c5:
        c.wait_send()
    for seg in range(3):
        all_of(r1[seg].at[pl.ds(1, 15)], p1s.at[seg])
        all_of(s2[seg].at[pl.ds(0, 7)], p2s.at[seg])
        all_of(out[seg].at[pl.ds(0, 15)], p4s.at[seg])
    all_of(t1.at[pl.ds(1, 15)], q1s)
    for c in kept:
        c.wait()


def run_main(x, u, gain, shift, wqkv, bqkv, wproj, table, maps):
    pw1, pw2, ps, ea, eb, er, hm = maps
    c = lambda a: jnp.asarray(a, bf16)
    S, s, D = pltpu.VMEM, jax.ShapeDtypeStruct, pltpu.SemaphoreType.DMA
    sems = [D((n,)) for n in (6, 6, 3, 3, 3, 3, 3, 3)] + [D(())] * 4 + [D((3,))] * 6
    j = jnp.asarray
    args = (x, u, c(ps), c(pw1), table, j(eb), j(ea), gain, shift, wqkv, bqkv, wproj, c(pw2), c(hm), c(pw2.T), c(pw1.T), j(er))
    outs = tuple(s((32, n, 16, 128), bf16) for n in (3, 3, 4)) + (s((392, 384), bf16), s((192, 384), bf16))
    return pl.pallas_call(
        main_kernel,
        out_shape=outs,
        in_specs=[pl.BlockSpec(memory_space=pltpu.HBM)] * 17,
        out_specs=(pl.BlockSpec(memory_space=pltpu.HBM),) * 5,
        scratch_shapes=[S(o.shape, o.dtype) for o in outs] + [D((5,))] + [S(a.shape, a.dtype) for a in args] + [D((17,))] + [
            S((392, 768), bf16), S((2, 192, 384), bf16), S((2, 192, 384), bf16),
            S((512, 384), f32), S((512, 1), f32), S((512, 384), bf16), S((512, 384), bf16),
            S((512, 1152), bf16), S((512, 384), bf16), S((512, 384), bf16), S((512, 1152), bf16),
            S((4, 3, 56, 256), f32), S((3, 56, 256), f32), S((16, 256), f32), S((48, 128), f32), S((512, 384), bf16),
            S((3, 32, 3, 16, 128), bf16), S((3, 16, 3, 16, 128), bf16), S((3, 16, 3, 16, 128), bf16),
        ] + [S((16, 3, 16, 128), bf16)] * 3 + [
            S((3, 3, 16, 128), f32), S((32, 16, 128), bf16), S((16, 16, 128), bf16), S((16, 16, 128), bf16),
            S((16, 16, 128), bf16), S((8, 128), f32),
        ] + [S((8, n, 16, 128), bf16) for n in (3, 3, 4)] + [S((192, 384), bf16)] + sems,
        compiler_params=pltpu.CompilerParams(collective_id=0, has_side_effects=True, vmem_limit_bytes=62 << 20),
    )(*args)


def final_kernel(
    scale, g0_in, g1_in, g2_in, u_in, gl_in, hr_in, q3_in,
    gx_o, wq_o, wp_o, a_out, b_out, bq_out, bp_out, t_out,
    g0, g1, g2, u, gl, hr, q3, load, gx, wq, wp, store, small, tab,
):
    pairs = ((g0_in, g0), (g1_in, g1), (g2_in, g2), (hr_in, hr), (q3_in, q3), (gl_in, gl), (u_in, u))
    loads = [pltpu.make_async_copy(a, b, load.at[i]) for i, (a, b) in enumerate(pairs)]
    for c in loads:
        c.start()
    stores = []

    def put(src, dst):
        c = pltpu.make_async_copy(src, dst, store.at[len(stores)])
        c.start()
        stores.append(c)

    for seg, g in enumerate((g0, g1, g2)):
        loads[seg].wait()
        for n in range(4):
            lb = 4 * seg + n
            dst, l = (wp, lb) if lb < 3 else (wq, lb - 3)
            for i in range(24):
                t = n * 24 + i
                dst[16 * i : 16 * i + 16, 128 * l : 128 * l + 128] = g[t // 3, t % 3].astype(f32) * scale
        lanes = (pl.ds(0, 128), pl.ds(128, 512), pl.ds(640, 512))[seg]
        put(wq.at[:, lanes], wq_o.at[:, lanes])
        if seg == 0:
            put(wp, wp_o)
    for c in loads[3:]:
        c.wait()
    got = gl[...].astype(f32) + dot(q3[...], hr[...])
    for p in range(196):
        gx[p] = (u[p].astype(f32) + got[2 * p : 2 * p + 2]).astype(bf16)
    put(gx, gx_o)
    for c in range(6):
        t = g2[c, 3].astype(f32)
        small[8 * c : 8 * c + 8] = (t[:8] + t[8:]) * scale
    for n in range(3):
        d = pl.ds(128 * n, 128)
        a_out[d] = small[n]
        b_out[d] = small[3 + n]
        bp_out[d] = small[15 + n]
    for n in range(9):
        bq_out[pl.ds(128 * n, 128)] = small[6 + n]
    tab[...] = jnp.zeros_like(tab)
    for h in range(12):
        tab[h : h + 1, 0:128] = small[18 + 2 * h : 19 + 2 * h]
        tab[h : h + 1, 128:256] = small[19 + 2 * h : 20 + 2 * h]
    t_out[...] = tab[0:12, 0:169]
    for c in stores:
        c.wait()


def run_final(scale, g0, g1, g2, u, gl, hr, maps):
    s = jax.ShapeDtypeStruct
    args = (g0, g1, g2, u, gl, hr, jnp.asarray(maps[2].T, bf16))
    big = (s((196, 2, 384), bf16), s((384, 1152), f32), s((384, 384), f32))
    return pl.pallas_call(
        functools.partial(final_kernel, scale),
        out_shape=big
        + (s((384,), f32), s((384,), f32), s((1152,), f32), s((384,), f32), s((12, 169), f32)),
        in_specs=[pl.BlockSpec(memory_space=pltpu.HBM)] * 7,
        out_specs=(pl.BlockSpec(memory_space=pltpu.HBM),) * 3 + (V,) * 5,
        scratch_shapes=[pltpu.VMEM(a.shape, a.dtype) for a in args]
        + [pltpu.SemaphoreType.DMA((7,))]
        + [pltpu.VMEM(a.shape, a.dtype) for a in big]
        + [pltpu.SemaphoreType.DMA((5,)), pltpu.VMEM((48, 128), f32), pltpu.VMEM((16, 256), f32)],
        compiler_params=pltpu.CompilerParams(vmem_limit_bytes=62 << 20),
    )(*args)


def on_device(features, grad_out, norm_gain, norm_shift, qkv_weight, qkv_bias, proj_weight, bias_table):
    maps = index_maps()
    x = features.transpose(1, 2, 0, 3).reshape(196, 2, 384)
    u = grad_out.transpose(1, 2, 0, 3).reshape(196, 2, 384)
    g0, g1, g2, gl, hr = run_main(x, u, norm_gain, norm_shift, qkv_weight, qkv_bias, proj_weight, bias_table.T, maps)
    scale = 1.0 / math.sqrt(8 * 112 * 112)
    gx, wq, wp, a, b, bq, bp, t = run_final(scale, g0, g1, g2, u, gl, hr, maps)
    return gx.reshape(14, 14, 2, 384).transpose(2, 0, 1, 3), a, b, wq, bq, wp, bp, t.T


def solution(mesh):
    return jax.shard_map(
        on_device,
        mesh=mesh,
        in_specs=(P("scene", "row", "col", None),) * 2 + (P(),) * 6,
        out_specs=(P("scene", "row", "col", None),) + (P(),) * 7,
        check_vma=False,
    )
```

```python
import functools
import math

import jax
import jax.numpy as jnp
import numpy as np
from jax import lax
from jax.experimental import pallas as pl
from jax.experimental.pallas import tpu as pltpu
from jax.sharding import PartitionSpec as P

WIN, SHIFT, NORM_EPS, MASKED = 7, 3, 1e-05, -1e30
LOG2E = 1.4426950408889634
UNROLL = 8
HIGH = lax.Precision.HIGHEST
MESH = pl.DeviceIdType.MESH
f32, bf16 = jnp.float32, jnp.bfloat16
V = pl.BlockSpec(memory_space=pltpu.VMEM)


def index_maps():
    pw1 = np.zeros((512, 392), np.float32)
    pw2 = np.zeros((512, 192), np.float32)
    ps = np.zeros((192, 392), np.float32)
    for s in range(2):
        for i in range(14):
            for j in range(14):
                w = (s * 2 + i // 7) * 2 + j // 7
                t = 64 * w + (i % 7) * 7 + j % 7
                flat = lambda a, b: (a * 14 + b) * 2 + s
                if i < 11 and j < 11:
                    pw1[t, flat(i + 3, j + 3)] = 1
                    continue
                if i >= 11 and j < 11:
                    slot, src = s * 33 + (i - 11) * 11 + j, flat(i - 11, j + 3)
                elif i < 11:
                    slot, src = 80 + s * 33 + i * 3 + j - 11, flat(i + 3, j - 11)
                else:
                    slot, src = 160 + s * 9 + (i - 11) * 3 + j - 11, flat(i - 11, j - 11)
                pw2[t, slot] = 1
                ps[slot, src] = 1
    ea = np.zeros((2, 128, 128), np.float32)
    eb = np.zeros((56, 96), np.float32)
    er = np.zeros((96, 56), np.float32)
    for a in range(49):
        off = (a // 7) * 13 + a % 7
        ea[0, off, a] = 1
        ea[1, off, 64 + a] = 1
        eb[a, off] = 1
        er[92 - off, a] = 1
    hm = (np.arange(256)[:, None] // 64 == np.arange(128)[None, :] // 32).astype(np.float32)
    return pw1, pw2, ps, ea, eb, er, hm


def place():
    row, z, scene = lax.axis_index("row"), lax.axis_index("col"), lax.axis_index("scene")
    x = (row // 4) * 2 + scene // 2
    return x, row % 4, z, scene % 2


def at(x, y, z, core):
    return ((x // 2) * 4 + y, z, (x % 2) * 2 + core)


def dot(a, b, ca=1, cb=0, **kw):
    return lax.dot_general(a, b, (((ca,), (cb,)), ((), ())), preferred_element_type=f32, **kw)


def split(t):
    hi = t.astype(bf16).astype(f32)
    return jnp.concatenate([hi, t - hi], axis=0).astype(bf16)


def main_kernel(
    x_in, u_in, ps_in, pw1_in, table_in, eb_in, ea_in, gain_in, shift_in, wqkv_in, bqkv_in, wproj_in, pw2_in, hm_in,
    q2_in, q1_in, er_in,
    out0_o, out1_o, out2_o, gl_o, hout_o,
    out0, out1, out2, gl, hout, store,
    x, u, ps, pw1, table, eb, ea, gain, shift, wqkv, bqkv, wproj, pw2, hm, q2, q1, er, load,
    flat, box, rx, xhat, rstd, norm, up, qkv, gat, attn, gq, tvar, gtab, tab, small, gsh,
    g, r0, s1, r1_0, r1_1, r1_2, acc, sg, t0, ts, t1, tacc, s2_0, s2_1, s2_2, hbox,
    hs, hr, bs, br, p0s, p0r, p1s, p1r, q0s, q0r, q1s, q1r, p2s, p2r, p4s, p4r, p5s, p5r,
):
    px, py, z, core = place()
    me = px * 4 + py
    row, scene = lax.axis_index("row"), lax.axis_index("scene")
    rm, zm = lax.rem(row + 7, 8), lax.rem(z + 7, 8)
    rp, zp = lax.rem(row + 1, 8), lax.rem(z + 1, 8)
    sib = at(px, py, z, 1 - core)

    def plane(k):
        return at(lax.rem(px + k // 4, 4), lax.rem(py + k % 4, 4), z, core)

    def depth(k):
        return at(px, py, lax.rem(z + k, 8), core)

    def send(src, dst, ss, rs, dev):
        return pltpu.make_async_remote_copy(
            src_ref=src, dst_ref=dst, send_sem=ss, recv_sem=rs, device_id=dev, device_id_type=MESH
        )

    bar = pltpu.get_barrier_semaphore()
    peers = [sib] + [plane(k) for k in range(1, 16)] + [depth(k) for k in range(1, 8)]
    peers += [(rm, zm, scene), (rp, zp, scene)]
    for d in peers:
        pl.semaphore_signal(bar, inc=1, device_id=d, device_id_type=MESH)

    loads = [
        pltpu.make_async_copy(a, b, load.at[i])
        for i, (a, b) in enumerate(
            (
                (x_in, x), (u_in, u), (ps_in, ps), (pw1_in, pw1), (table_in, table), (eb_in, eb), (ea_in, ea),
                (gain_in, gain), (shift_in, shift), (wqkv_in, wqkv), (bqkv_in, bqkv), (wproj_in, wproj),
                (pw2_in, pw2), (hm_in, hm), (q2_in, q2), (q1_in, q1), (er_in, er),
            )
        )
    ]
    for c in loads:
        c.start()
    for c in loads[:3]:
        c.wait()
    for p in range(196):
        flat[2 * p : 2 * p + 2, 0:384] = x[p]
        flat[2 * p : 2 * p + 2, 384:768] = u[p]
    box[0] = dot(ps[...], flat[:, 0:384]).astype(bf16)
    box[1] = dot(ps[...], flat[:, 384:768]).astype(bf16)
    pl.semaphore_wait(bar, len(peers))
    pieces = ((0, 80), (80, 80), (160, 32))
    halo = []
    for h in range(2):
        for i, (d, (lo, n)) in enumerate(zip(((rm, z, scene), (row, zm, scene), (rm, zm, scene)), pieces)):
            i = 3 * h + i
            c = send(box.at[h, pl.ds(lo, n)], rx.at[h, pl.ds(lo, n)], hs.at[i], hr.at[i], d)
            c.start()
            halo.append(c)
    for c in loads[3:]:
        c.wait()

    tab[...] = jnp.zeros_like(tab)
    tab[0:12, 0:169] = table[...] * LOG2E
    heads = pltpu.roll(tab[...], 4, 1)
    for pair in range(6):
        parts = []
        for half in range(2):
            h = 2 * pair + half
            wide = jnp.broadcast_to(heads[h : h + 1], (96, 256))
            wide = pltpu.roll(wide, 168, 1, stride=1, stride_axis=0)[:, :128]
            rows = dot(eb[...], wide, precision=HIGH)
            parts.append(dot(rows, ea[half], precision=HIGH))
        lo = (pair % 2) * 128
        tvar[0, pair // 2, :, lo : lo + 128] = parts[0] + parts[1]
    key = lax.broadcasted_iota(jnp.int32, (56, 256), 0)
    query = lax.broadcasted_iota(jnp.int32, (56, 256), 1) & 63

    def low(t):
        return (t >= 28).astype(jnp.int32), ((t - 7 * ((t * 37) >> 8)) >= 4).astype(jnp.int32)

    (ky, kx), (qy, qx_) = low(key), low(query)
    pad = key >= 49
    bad_row = ((ky != qy) & (query < 49)) & (row == 7)
    bad_col = ((kx != qx_) & (query < 49)) & (z == 7)
    for grp in range(3):
        t = jnp.where(pad, MASKED, tvar[0, grp])
        tvar[0, grp] = t
        tr = jnp.where(bad_row, MASKED, t)
        tvar[1, grp] = jnp.where(bad_col, MASKED, t)
        tvar[2, grp] = tr
        tvar[3, grp] = jnp.where(bad_col, MASKED, tr)
    gtab[...] = jnp.zeros_like(gtab)
    gq[...] = jnp.zeros_like(gq)

    v = dot(pw1[...], flat[:, 0:384])
    for c in halo[:3]:
        c.wait_recv()
    v = v + dot(pw2[...], rx[0])
    cen = v - jnp.sum(v, axis=1, keepdims=True) * (1.0 / 384)
    inv = lax.rsqrt(jnp.sum(cen * cen, axis=1, keepdims=True) * (1.0 / 384) + NORM_EPS)
    rstd[...] = inv
    xh = cen * inv
    xhat[...] = xh
    norm[...] = (xh * gain[...].reshape(1, 384) + shift[...].reshape(1, 384)).astype(bf16)
    for n in range(3):
        lanes = slice(384 * n, 384 * n + 384)
        qkv[:, lanes] = (dot(norm[...], wqkv[:, lanes]) + bqkv[...].reshape(1, 1152)[:, lanes]).astype(bf16)
    v = dot(pw1[...], flat[:, 384:768])
    for c in halo[3:]:
        c.wait_recv()
    up[...] = (v + dot(pw2[...], rx[1])).astype(bf16)
    gat[...] = dot(up[...], wproj[...], 1, 1).astype(bf16)

    scale = 32**-0.5
    lane = lax.broadcasted_iota(jnp.int32, (64, 128), 1)

    def merge(r):
        return jnp.where(
            lane < 32, r[0:64], jnp.where(lane < 64, r[64:128], jnp.where(lane < 96, r[128:192], r[192:256]))
        )

    def window(w, carry):
        base = pl.multiple_of(w * 64, 64)
        var = lax.rem(w, 4)
        for grp in range(3):
            lanes = [slice(384 * n + 128 * grp, 384 * n + 128 * grp + 128) for n in range(3)]
            q = qkv[pl.ds(base, 64), lanes[0]]
            k = qkv[pl.ds(base, 56), lanes[1]]
            vv = qkv[pl.ds(base, 56), lanes[2]]
            ga = gat[pl.ds(base, 64), lanes[0]]
            qx = jnp.concatenate([q, q, q, q], axis=0) * hm[...]
            gx = jnp.concatenate([ga, ga, ga, ga], axis=0) * hm[...]
            s = dot(k, qx, 1, 1) * (scale * LOG2E) + tvar[var, grp]
            e = jnp.exp2(s - jnp.max(s, axis=0, keepdims=True))
            p = e * (1.0 / jnp.sum(e, axis=0, keepdims=True))
            pb = p.astype(bf16)
            attn[pl.ds(base, 64), lanes[0]] = merge(dot(pb, vv, 0, 0)).astype(bf16)
            dp = dot(vv, gx, 1, 1)
            ds = p * (dp - jnp.sum(dp * p, axis=0, keepdims=True))
            gtab[grp] += ds
            db = ds.astype(bf16)
            gq[pl.ds(base, 64), lanes[0]] = (merge(dot(db, k, 0, 0)) * scale).astype(bf16)
            gq[pl.ds(base, 56), lanes[1]] = (dot(db, qx) * scale).astype(bf16)
            gq[pl.ds(base, 56), lanes[2]] = dot(pb, gx).astype(bf16)
        return carry

    def windows(i, carry):
        for j in range(UNROLL):
            window(i * UNROLL + j, carry)
        return carry

    lax.fori_loop(0, 8 // UNROLL, windows, 0)

    out, r1, s2 = (out0, out1, out2), (r1_0, r1_1, r1_2), (s2_0, s2_1, s2_2)
    hops = lambda k: min(k // 4, 4 - k // 4) + min(k % 4, 4 - k % 4)
    order = sorted(range(16), key=hops, reverse=True)
    far = (4, 3, 5, 2, 6, 1, 7)
    c0, c5 = [], []

    def all_of(what, sem):
        pltpu.make_async_copy(what, what, sem).wait()

    def chunk(k):
        return lax.rem(px + k // 4, 4) * 4 + lax.rem(py + k % 4, 4)

    for seg in range(3):
        for n in range(4):
            lb = 4 * seg + n
            if lb < 3:
                m = dot(attn[...], up[:, 128 * lb : 128 * lb + 128], 0, 0)
            else:
                m = dot(norm[...], gq[:, 128 * (lb - 3) : 128 * (lb - 3) + 128], 0, 0)
            for i in range(24):
                t = n * 24 + i
                g[seg, t // 3, t % 3] = m[16 * i : 16 * i + 16].astype(bf16)
        c = send(g.at[seg, pl.ds((1 - core) * 16, 16)], r0.at[seg], p0s.at[seg], p0r.at[seg], sib)
        c.start()
        c0.append(c)

    def spread(seg):
        c0[seg].wait_recv()
        for k in order:
            c = chunk(k)
            total = g[seg, core * 16 + c].astype(f32) + r0[seg, c].astype(f32)
            if k:
                s1[seg, c] = total.astype(bf16)
                c = send(s1.at[seg, c], r1[seg].at[k], p1s.at[seg], p1r.at[seg], plane(k))
                c.start()
            else:
                acc[seg] = total

    def deepen(seg):
        a = acc[seg]
        all_of(r1[seg].at[pl.ds(1, 15)], p1r.at[seg])
        for k in range(1, 16):
            a = a + r1[seg][k].astype(f32)
        s2[seg][z, 0:3] = a.astype(bf16)
        if seg == 2:
            all_of(t1.at[pl.ds(1, 15)], q1r)
            for k in range(1, 16):
                t = t1[k].astype(f32)
                tacc[...] += t[:8] + t[8:]
            s2[seg][z, 3] = split(tacc[...])
        for k in far:
            c = send(s2[seg].at[z], s2[seg].at[z], p2s.at[seg], p2r.at[seg], depth(k))
            c.start()

    mine = core * 16 + me

    def finish(seg):
        all_of(s2[seg].at[pl.ds(0, 7)], p2r.at[seg])
        a = s2[seg][0].astype(f32)
        for t in range(1, 8):
            a = a + s2[seg][t].astype(f32)
        out[seg][mine, 0:3] = a[0:3].astype(bf16)
        if seg == 2:
            out[seg][mine, 3] = split(a[3, :8] + a[3, 8:])
        for k in order[:15]:
            c = send(out[seg].at[mine], out[seg].at[mine], p4s.at[seg], p4r.at[seg], plane(k))
            c.start()

    def hand_over(seg):
        all_of(out[seg].at[pl.ds(0, 15)], p4r.at[seg])
        half = pl.ds(core * 16, 16)
        c = send(out[seg].at[half], out[seg].at[half], p5s.at[seg], p5r.at[seg], sib)
        c.start()
        c5.append(c)

    def keep(i, src, dst):
        c = pltpu.make_async_copy(src, dst, store.at[i])
        c.start()
        kept.append(c)

    kept = []
    spread(0)

    gn = dot(gq[...], wqkv[...], 1, 1).astype(bf16).astype(f32)
    xh = xhat[...]
    spread(1)
    spread(2)
    a = jnp.sum(gn * xh, axis=0, keepdims=True)
    b = jnp.sum(gn, axis=0, keepdims=True)
    for n in range(3):
        small[n : n + 1] = a[:, 128 * n : 128 * n + 128]
        small[3 + n : 4 + n] = b[:, 128 * n : 128 * n + 128]

    ones = jnp.ones((16, 512), bf16)
    sq = dot(ones, gq[...])[0:1]
    sp = dot(ones, up[...])[0:1]
    for n in range(9):
        small[6 + n : 7 + n] = sq[:, 128 * n : 128 * n + 128]
    for n in range(3):
        small[15 + n : 16 + n] = sp[:, 128 * n : 128 * n + 128]
    d = jnp.concatenate([gtab[p // 2, :, (p % 2) * 128 : (p % 2) * 128 + 128] for p in range(6)], axis=0)
    hi = d.astype(bf16)
    lo = (d - hi.astype(f32)).astype(bf16)
    eab = jnp.concatenate([ea[0], ea[1]], axis=0).astype(bf16)
    erb = er[...].astype(bf16)
    hi, lo = dot(hi, eab, 1, 1).astype(bf16), dot(lo, eab, 1, 1).astype(bf16)
    for pair in range(6):
        rows = slice(56 * pair, 56 * pair + 56)
        r = dot(erb, hi[rows]) + dot(erb, lo[rows])
        for half in range(2):
            h = 2 * pair + half
            wide = jnp.concatenate([r[:, 128 * half : 128 * half + 128], jnp.zeros((96, 128), f32)], axis=1)
            wide = pltpu.roll(wide, 248, 1, stride=1, stride_axis=0)
            u_h = jnp.sum(wide, axis=0, keepdims=True)
            small[18 + 2 * h : 19 + 2 * h] = u_h[:, :128]
            small[19 + 2 * h : 20 + 2 * h] = u_h[:, 128:]
    small[42:48] = jnp.zeros((6, 128), f32)
    for c in range(32):
        sg[c] = split(small[8 * c : 8 * c + 8]) if c < 6 else jnp.zeros((16, 128), bf16)
    d0 = send(sg.at[pl.ds((1 - core) * 16, 16)], t0, q0s, q0r, sib)
    d0.start()
    deepen(0)
    d0.wait_recv()
    for k in order:
        c = chunk(k)
        total = sg[core * 16 + c].astype(f32) + t0[c].astype(f32)
        total = total[:8] + total[8:]
        if k:
            ts[c] = split(total)
            c = send(ts.at[c], t1.at[k], q1s, q1r, plane(k))
            c.start()
        else:
            tacc[...] = total
    deepen(1)
    gg = gn * gain[...].reshape(1, 384)
    m1 = jnp.sum(gg, axis=1, keepdims=True) * (1.0 / 384)
    m2 = jnp.sum(gg * xh, axis=1, keepdims=True) * (1.0 / 384)
    gsh[...] = ((gg - m1 - xh * m2) * rstd[...]).astype(bf16)
    hbox[...] = dot(q2[...], gsh[...]).astype(bf16)
    back = []
    for i, (d, (lo, n)) in enumerate(zip(((rp, z, scene), (row, zp, scene), (rp, zp, scene)), pieces)):
        c = send(hbox.at[pl.ds(lo, n)], hout.at[pl.ds(lo, n)], bs.at[i], br.at[i], d)
        c.start()
        back.append(c)
    gl[...] = dot(q1[...], gsh[...]).astype(bf16)

    keep(3, gl, gl_o)
    finish(0)
    deepen(2)
    finish(1)
    finish(2)
    hand_over(0)
    hand_over(1)
    for c in back:
        c.wait_recv()
    keep(4, hout, hout_o)
    half, other = pl.ds(core * 16, 16), pl.ds((1 - core) * 16, 16)
    send(out0.at[half], out0.at[other], p5s.at[0], p5r.at[0], sib).wait_recv()
    keep(0, out0, out0_o)
    hand_over(2)
    send(out1.at[half], out1.at[other], p5s.at[1], p5r.at[1], sib).wait_recv()
    keep(1, out1, out1_o)
    send(out2.at[half], out2.at[other], p5s.at[2], p5r.at[2], sib).wait_recv()
    keep(2, out2, out2_o)
    for c in halo + back + c0 + [d0] + c5:
        c.wait_send()
    for seg in range(3):
        all_of(r1[seg].at[pl.ds(1, 15)], p1s.at[seg])
        all_of(s2[seg].at[pl.ds(0, 7)], p2s.at[seg])
        all_of(out[seg].at[pl.ds(0, 15)], p4s.at[seg])
    all_of(t1.at[pl.ds(1, 15)], q1s)
    for c in kept:
        c.wait()


def run_main(x, u, gain, shift, wqkv, bqkv, wproj, table, maps):
    pw1, pw2, ps, ea, eb, er, hm = maps
    c = lambda a: jnp.asarray(a, bf16)
    S, s, D = pltpu.VMEM, jax.ShapeDtypeStruct, pltpu.SemaphoreType.DMA
    sems = [D((n,)) for n in (6, 6, 3, 3, 3, 3, 3, 3)] + [D(())] * 4 + [D((3,))] * 6
    j = jnp.asarray
    args = (x, u, c(ps), c(pw1), table, j(eb), j(ea), gain, shift, wqkv, bqkv, wproj, c(pw2), c(hm), c(pw2.T), c(pw1.T), j(er))
    outs = tuple(s((32, n, 16, 128), bf16) for n in (3, 3, 4)) + (s((392, 384), bf16), s((192, 384), bf16))
    return pl.pallas_call(
        main_kernel,
        out_shape=outs,
        in_specs=[pl.BlockSpec(memory_space=pltpu.HBM)] * 17,
        out_specs=(pl.BlockSpec(memory_space=pltpu.HBM),) * 5,
        scratch_shapes=[S(o.shape, o.dtype) for o in outs] + [D((5,))] + [S(a.shape, a.dtype) for a in args] + [D((17,))] + [
            S((392, 768), bf16), S((2, 192, 384), bf16), S((2, 192, 384), bf16),
            S((512, 384), f32), S((512, 1), f32), S((512, 384), bf16), S((512, 384), bf16),
            S((512, 1152), bf16), S((512, 384), bf16), S((512, 384), bf16), S((512, 1152), bf16),
            S((4, 3, 56, 256), f32), S((3, 56, 256), f32), S((16, 256), f32), S((48, 128), f32), S((512, 384), bf16),
            S((3, 32, 3, 16, 128), bf16), S((3, 16, 3, 16, 128), bf16), S((3, 16, 3, 16, 128), bf16),
        ] + [S((16, 3, 16, 128), bf16)] * 3 + [
            S((3, 3, 16, 128), f32), S((32, 16, 128), bf16), S((16, 16, 128), bf16), S((16, 16, 128), bf16),
            S((16, 16, 128), bf16), S((8, 128), f32),
        ] + [S((8, n, 16, 128), bf16) for n in (3, 3, 4)] + [S((192, 384), bf16)] + sems,
        compiler_params=pltpu.CompilerParams(collective_id=0, has_side_effects=True, vmem_limit_bytes=62 << 20),
    )(*args)


def final_kernel(
    scale, g0_in, g1_in, g2_in, u_in, gl_in, hr_in, q3_in,
    gx_o, wq_o, wp_o, a_out, b_out, bq_out, bp_out, t_out,
    g0, g1, g2, u, gl, hr, q3, load, gx, wq, wp, store, small, tab,
):
    pairs = ((g0_in, g0), (g1_in, g1), (g2_in, g2), (hr_in, hr), (q3_in, q3), (gl_in, gl), (u_in, u))
    loads = [pltpu.make_async_copy(a, b, load.at[i]) for i, (a, b) in enumerate(pairs)]
    for c in loads:
        c.start()
    stores = []

    def put(src, dst):
        c = pltpu.make_async_copy(src, dst, store.at[len(stores)])
        c.start()
        stores.append(c)

    for seg, g in enumerate((g0, g1, g2)):
        loads[seg].wait()
        for n in range(4):
            lb = 4 * seg + n
            dst, l = (wp, lb) if lb < 3 else (wq, lb - 3)
            for i in range(24):
                t = n * 24 + i
                dst[16 * i : 16 * i + 16, 128 * l : 128 * l + 128] = g[t // 3, t % 3].astype(f32) * scale
        lanes = (pl.ds(0, 128), pl.ds(128, 512), pl.ds(640, 512))[seg]
        put(wq.at[:, lanes], wq_o.at[:, lanes])
        if seg == 0:
            put(wp, wp_o)
    for c in loads[3:]:
        c.wait()
    got = gl[...].astype(f32) + dot(q3[...], hr[...])
    for p in range(196):
        gx[p] = (u[p].astype(f32) + got[2 * p : 2 * p + 2]).astype(bf16)
    put(gx, gx_o)
    for c in range(6):
        t = g2[c, 3].astype(f32)
        small[8 * c : 8 * c + 8] = (t[:8] + t[8:]) * scale
    for n in range(3):
        d = pl.ds(128 * n, 128)
        a_out[d] = small[n]
        b_out[d] = small[3 + n]
        bp_out[d] = small[15 + n]
    for n in range(9):
        bq_out[pl.ds(128 * n, 128)] = small[6 + n]
    tab[...] = jnp.zeros_like(tab)
    for h in range(12):
        tab[h : h + 1, 0:128] = small[18 + 2 * h : 19 + 2 * h]
        tab[h : h + 1, 128:256] = small[19 + 2 * h : 20 + 2 * h]
    t_out[...] = tab[0:12, 0:169]
    for c in stores:
        c.wait()


def run_final(scale, g0, g1, g2, u, gl, hr, maps):
    s = jax.ShapeDtypeStruct
    args = (g0, g1, g2, u, gl, hr, jnp.asarray(maps[2].T, bf16))
    big = (s((196, 2, 384), bf16), s((384, 1152), f32), s((384, 384), f32))
    return pl.pallas_call(
        functools.partial(final_kernel, scale),
        out_shape=big
        + (s((384,), f32), s((384,), f32), s((1152,), f32), s((384,), f32), s((12, 169), f32)),
        in_specs=[pl.BlockSpec(memory_space=pltpu.HBM)] * 7,
        out_specs=(pl.BlockSpec(memory_space=pltpu.HBM),) * 3 + (V,) * 5,
        scratch_shapes=[pltpu.VMEM(a.shape, a.dtype) for a in args]
        + [pltpu.SemaphoreType.DMA((7,))]
        + [pltpu.VMEM(a.shape, a.dtype) for a in big]
        + [pltpu.SemaphoreType.DMA((5,)), pltpu.VMEM((48, 128), f32), pltpu.VMEM((16, 256), f32)],
        compiler_params=pltpu.CompilerParams(vmem_limit_bytes=62 << 20),
    )(*args)


def on_device(features, grad_out, norm_gain, norm_shift, qkv_weight, qkv_bias, proj_weight, bias_table):
    maps = index_maps()
    x = features.transpose(1, 2, 0, 3).reshape(196, 2, 384)
    u = grad_out.transpose(1, 2, 0, 3).reshape(196, 2, 384)
    g0, g1, g2, gl, hr = run_main(x, u, norm_gain, norm_shift, qkv_weight, qkv_bias, proj_weight, bias_table.T, maps)
    scale = 1.0 / math.sqrt(8 * 112 * 112)
    gx, wq, wp, a, b, bq, bp, t = run_final(scale, g0, g1, g2, u, gl, hr, maps)
    return gx.reshape(14, 14, 2, 384).transpose(2, 0, 1, 3), a, b, wq, bq, wp, bp, t.T


def solution(mesh):
    return jax.shard_map(
        on_device,
        mesh=mesh,
        in_specs=(P("scene", "row", "col", None),) * 2 + (P(),) * 6,
        out_specs=(P("scene", "row", "col", None),) + (P(),) * 7,
        check_vma=False,
    )
```
